256 devices in a mesh: dp: 8 (over x, z_lo), tensor: 32 (over y, z_hi, core).
Axes of the slice: x: 4, y: 4, z: 8 (z_hi: 4, z_lo: 2; z = z_hi * 2 + z_lo), core: 2. Of those that a mesh axis runs over, the one named last changes fastest.
Arguments:
- text: bfloat16 [2048, 8192], P('dp', 'tensor'), may hold values from -6 to 6
- grad_out: bfloat16 [2048, 8192], P('dp', 'tensor'), may hold values from -6 to 6
- vision: bfloat16 [2048, 7680], P('dp', 'tensor'), may hold values from -32 to 32
- gate: float32 [1], replicated, may hold values from 0.3 to 1.5
- w_query: bfloat16 [8192, 8192], P('dp', 'tensor'), may hold values from -0.0625 to 0.0625
- w_key: bfloat16 [7680, 1024], P('tensor', 'dp'), may hold values from -0.0625 to 0.0625
- w_value: bfloat16 [7680, 1024], P('tensor', 'dp'), may hold values from -0.0625 to 0.0625
- w_out: bfloat16 [8192, 8192], P('tensor', 'dp'), may hold values from -0.0625 to 0.0625
Outputs:
- update: bfloat16 [2048, 8192], P('dp', 'tensor')
- grad_text: bfloat16 [2048, 8192], P('dp', 'tensor')
- grad_vision: bfloat16 [2048, 7680], P('dp', 'tensor')
The draws below stay inside these ranges and needn't reach their ends.
All inputs are finite; a program needn't handle non-finite values.
Results may differ from the reference program's by a relative error of at most 0.034.
Values may be sent and summed in bfloat16 or wider, within the bound.
A program may use at most 64 MiB of HBM per device.

```python
import jax
import jax.numpy as jnp
from jax import lax

D = 8192
HEADS = 64
KV_HEADS = 8
HEAD = 128
DV = 7680
TOK = 256
VROWS = 256
TOKENS = 2048
VISION = 2048
N_DP = 8
N_TENSOR = 32


def with_spikes(drawn, own_key, source, target, parts, factor):
    def block_of(dim):
        return (jnp.arange(drawn.shape[dim]) // (drawn.shape[dim] // parts)).reshape((-1,) + (1,) * (drawn.ndim - 1 - dim))

    first = jax.random.permutation(own_key, parts)[block_of(target)]
    other_side = (block_of(target) + parts // 2) % parts
    return jnp.where((block_of(source) == first) | (block_of(source) == other_side), factor * drawn, drawn)


def block_scale(rng, extent, cuts, smallest, top_value):
    def one(position, parts):
        heights = jax.random.uniform(jax.random.fold_in(jax.random.fold_in(rng, 6), position), (parts,), jnp.float32, smallest / len(cuts), top_value / len(cuts))
        return jnp.repeat(jnp.exp(heights), extent[position] // parts).reshape((-1,) + (1,) * (len(extent) - position - 1))

    loudness = one(*cuts[0])
    for cut in cuts[1:]:
        loudness = loudness * one(*cut)
    return loudness


def gaussian(key, shape, scale, most, pieces=(), kind=jnp.bfloat16):
    values = scale * jax.random.normal(key, shape, jnp.float32)
    if pieces:
        values = values * block_scale(key, shape, pieces, -0.22, 0.18)
    return jnp.clip(values, -most, most).astype(kind)


def bell_draw_with(key, shape, scale, bound, pieces, heavy, kind=jnp.bfloat16):
    result = scale * jax.random.normal(key, shape, jnp.float32)
    if pieces:
        result = result * block_scale(key, shape, pieces, -0.22, 0.18)
    return jnp.clip(with_spikes(result, jax.random.fold_in(key, 3), *heavy), -bound, bound).astype(kind)


def setup_inputs(seed: int = 0) -> dict:
    seeds = jax.random.split(jax.random.key(seed), 9)
    text = gaussian(seeds[0], (TOKENS, D), 1.0, 6.0, ((0, 8), (1, 32)))
    grad_out = gaussian(seeds[1], (TOKENS, D), 1.0, 6.0, ((0, 8), (1, 32)))
    vision = bell_draw_with(seeds[2], (VISION, DV), 3.0, 32.0, ((0, 8), (1, 32)), (1, 0, 32, 2.75))
    gate = jnp.clip(jax.random.uniform(seeds[3], (1,), jnp.float32, 0.3, 1.5), 0.3, 1.5)
    w_query = gaussian(seeds[4], (D, HEADS * HEAD), D ** -0.5, 0.0625, ((0, 8), (1, 32)))
    w_key = gaussian(seeds[5], (DV, KV_HEADS * HEAD), DV ** -0.5, 0.0625, ((0, 32), (1, 8)))
    w_value = gaussian(seeds[6], (DV, KV_HEADS * HEAD), DV ** -0.5, 0.0625, ((0, 32), (1, 8)))
    w_out = gaussian(seeds[7], (HEADS * HEAD, D), (HEADS * HEAD) ** -0.5, 0.0625, ((0, 32), (1, 8)))
    return {"text": text, "grad_out": grad_out, "vision": vision, "gate": gate, "w_query": w_query, "w_key": w_key, "w_value": w_value, "w_out": w_out}


EPS = 1e-05

def rms_scale(tensor_in):
    return lax.rsqrt(lax.optimization_barrier(jnp.mean(tensor_in * tensor_in, axis=-1, keepdims=True)) + EPS)

def to_low(tensor_in):
    return lax.optimization_barrier(tensor_in.astype(jnp.bfloat16)).astype(jnp.float32)

def reference(text, grad_out, vision, gate, w_query, w_key, w_value, w_out):
    gate_tanh = jnp.tanh(gate[0])
    per_device = HEADS // N_TENSOR
    per_head = N_TENSOR // KV_HEADS
    width = per_device * HEAD
    scale = HEAD ** (-0.5)

    def sample(inputs):
        text_rows, grad_rows, vision_rows = inputs
        keys = jnp.dot(vision_rows, w_key, preferred_element_type=jnp.float32).reshape(VROWS, KV_HEADS, HEAD)
        key_scale = rms_scale(keys)
        key_normed = (keys * key_scale).astype(jnp.bfloat16)
        values = jnp.dot(vision_rows, w_value, preferred_element_type=jnp.float32).astype(jnp.bfloat16).reshape(VROWS, KV_HEADS, HEAD)
        query = jnp.dot(text_rows, w_query, preferred_element_type=jnp.float32).reshape(TOK, HEADS, HEAD)
        query_scale = rms_scale(query)
        query_normed = (query * query_scale).astype(jnp.bfloat16)

        def group(carry, index):
            out_sum, input_sum, kv_grads = carry
            start = index * per_device
            kv_index = index // per_head
            q_group = lax.dynamic_slice_in_dim(query_normed, start, per_device, 1).astype(jnp.float32)
            q_raw = lax.dynamic_slice_in_dim(query, start, per_device, 1)
            q_scale = lax.dynamic_slice_in_dim(query_scale, start, per_device, 1)
            key_head = lax.dynamic_index_in_dim(key_normed, kv_index, 1, keepdims=False).astype(jnp.float32)
            value_head = lax.dynamic_index_in_dim(values, kv_index, 1, keepdims=False).astype(jnp.float32)
            scores = jnp.einsum('thd,rd->thr', q_group, key_head) * scale
            expo = jnp.exp(scores)
            probs = expo / lax.optimization_barrier(jnp.sum(expo, axis=-1, keepdims=True))
            probs_low = probs.astype(jnp.bfloat16).astype(jnp.float32)
            attended = jnp.einsum('thr,rd->thd', probs_low, value_head).astype(jnp.bfloat16).reshape(TOK, width)
            out_rows = lax.dynamic_slice_in_dim(w_out, index * width, width, 0)
            out_part = to_low(jnp.dot(attended, out_rows, preferred_element_type=jnp.float32))
            attend_grad = (gate_tanh * jnp.dot(grad_rows, out_rows.T, preferred_element_type=jnp.float32)).astype(jnp.bfloat16)
            attend_grad = attend_grad.reshape(TOK, per_device, HEAD).astype(jnp.float32)
            prob_grad = jnp.einsum('thd,rd->thr', attend_grad, value_head)
            delta = lax.optimization_barrier(jnp.sum(probs * prob_grad, axis=-1, keepdims=True))
            score_grad = (probs * (prob_grad - delta) * scale).astype(jnp.bfloat16).astype(jnp.float32)
            normed_grad = jnp.einsum('thr,rd->thd', score_grad, key_head)
            query_grad = q_scale * normed_grad - q_raw * q_scale ** 3 * lax.optimization_barrier(jnp.mean(normed_grad * q_raw, axis=-1, keepdims=True))
            query_grad = query_grad.astype(jnp.bfloat16).reshape(TOK, width)
            query_cols = lax.dynamic_slice_in_dim(w_query, index * width, width, 1)
            input_part = to_low(jnp.dot(query_grad, query_cols.T, preferred_element_type=jnp.float32))
            key_part = jnp.einsum('thr,thd->rd', score_grad, q_group)
            value_part = jnp.einsum('thr,thd->rd', probs_low, attend_grad)
            kv_part = to_low(jnp.stack((key_part, value_part), 1))
            current = lax.dynamic_index_in_dim(kv_grads, kv_index, 1, keepdims=False)
            kv_grads = lax.dynamic_update_index_in_dim(kv_grads, current + kv_part, kv_index, 1)
            return ((out_sum + out_part, input_sum + input_part, kv_grads), None)
        start_carry = (jnp.zeros((TOK, D), jnp.float32), jnp.zeros((TOK, D), jnp.float32), jnp.zeros((VROWS, KV_HEADS, 2, HEAD), jnp.float32))
        carry, _ = lax.scan(group, start_carry, jnp.arange(N_TENSOR, dtype=jnp.int32))
        out_sum, input_sum, kv_grads = carry
        update = (gate_tanh * out_sum).astype(jnp.bfloat16)
        grad_text = input_sum.astype(jnp.bfloat16)
        key_side = kv_grads[:, :, 0]
        key_grad = key_scale * key_side - keys * key_scale ** 3 * lax.optimization_barrier(jnp.mean(key_side * keys, axis=-1, keepdims=True))
        key_grad = key_grad.astype(jnp.bfloat16).reshape(VROWS, KV_HEADS * HEAD)
        value_grad = kv_grads[:, :, 1].astype(jnp.bfloat16).reshape(VROWS, KV_HEADS * HEAD)
        grad_vision = (jnp.dot(key_grad, w_key.T, preferred_element_type=jnp.float32) + jnp.dot(value_grad, w_value.T, preferred_element_type=jnp.float32)).astype(jnp.bfloat16)
        return (update, grad_text, grad_vision)
    update, grad_text, grad_vision = lax.map(sample, (text.reshape(N_DP, TOK, D), grad_out.reshape(N_DP, TOK, D), vision.reshape(N_DP, VROWS, DV)))
    return (update.reshape(TOK * N_DP, D), grad_text.reshape(TOK * N_DP, D), grad_vision.reshape(VROWS * N_DP, DV))
```

```python
import jax
import jax.numpy as jnp
from jax import lax
from jax.experimental import pallas as pl
from jax.experimental.pallas import tpu as pltpu
from jax.sharding import PartitionSpec as P

HEAD = 128
EPS = 1e-05
MESH = pl.DeviceIdType.MESH
F32 = jnp.float32
BF16 = jnp.bfloat16
OFFSETS = (0, 3, 1, 2)
NT = (((1,), (1,)), ((), ()))
TN = (((0,), (0,)), ((), ()))


def dot(a, b, dims=(((1,), (0,)), ((), ()))):
    return lax.dot_general(a, b, dims, preferred_element_type=F32)


class Here:
    def __init__(self):
        d, t = lax.axis_index("dp"), lax.axis_index("tensor")
        self.x, self.zl = d // 2, d % 2
        self.y, self.zh, self.c = t // 8, (t // 2) % 4, t % 2
        self.z = 2 * self.zh + self.zl
        self.half = self.zh // 2

    def at(self, dx=0, dy=0, z=None, c=None):
        x = (self.x + dx) % 4 if dx else self.x
        y = (self.y + dy) % 4 if dy else self.y
        z = self.z if z is None else z
        c = self.c if c is None else c
        return (x * 2 + z % 2, y * 8 + (z // 2) * 2 + c)


def rcopy(src, dst, send, recv, device):
    return pltpu.make_async_remote_copy(
        src_ref=src, dst_ref=dst, send_sem=send, recv_sem=recv, device_id=device, device_id_type=MESH
    )


class Sends:
    def __init__(self):
        self.waits = []

    def start(self, *args):
        copy = rcopy(*args)
        copy.start()
        self.waits.append(copy.wait_send)

    def start_unless_self(self, me, z, src, dst, send, recv, device):
        @pl.when(z != me.z)
        def _():
            rcopy(src, dst, send, recv, device).start()

        @pl.when(z == me.z)
        def _():
            pltpu.make_async_copy(src, dst, recv).start()

        def finish():
            @pl.when(z != me.z)
            def _():
                rcopy(src, dst, send, recv, device).wait_send()

        self.waits.append(finish)

    def finish(self):
        for wait in self.waits:
            wait()


def arrived(dst, sem):
    pltpu.make_async_copy(dst, dst, sem).wait()


class RingGather:
    def __init__(self, me, sends, own, buf, cut, sems):
        self.me, self.sends, self.own, self.buf, self.cut = me, sends, own, buf, cut
        self.ss, self.rs = sems

    def start(self):
        me = self.me
        for way, dx in enumerate((1, -1)):
            self.sends.start(self.own, self.buf.at[me.x], self.ss.at[way], self.rs.at[way], me.at(dx=dx))

    def part(self, slot, way):
        rows = self.buf.shape[1]
        lo, n = ((0, self.cut), (self.cut, rows - self.cut))[way]
        return self.buf.at[slot, pl.ds(lo, n)]

    def relay(self, way):
        me, dx = self.me, (1, -1)[way]
        slot = (me.x - dx) % 4
        arrived(self.buf.at[slot], self.rs.at[way])
        block = self.part(slot, way)
        self.sends.start(block, block, self.ss.at[2 + way], self.rs.at[2 + way], me.at(dx=dx))

    def finish(self):
        for way in range(2):
            arrived(self.part((self.me.x + 2) % 4, way), self.rs.at[2 + way])


class Gather:
    def __init__(self, me, sends, own, buf, sems):
        self.me, self.sends, self.own, self.buf = me, sends, own, buf
        self.zs, self.zr, self.ys, self.yr, self.cs, self.cr = sems

    def start_z(self):
        me = self.me
        dst = self.buf.at[me.y, me.zh % 2, me.c, me.zl]
        recv = self.zr.at[(me.zh % 2) * 2 + me.zl]
        for i in range(4):
            z = me.half + 2 * i
            self.sends.start_unless_self(me, z, self.own, dst, self.zs.at[i], recv, me.at(z=z))

    def to_core(self, slot, r, k):
        me = self.me
        block = self.buf.at[slot, k, me.c]
        self.sends.start(block, block, self.cs.at[r * 2 + k], self.cr.at[r * 2 + k], me.at(c=1 - me.c))

    def start_y(self, k):
        me = self.me
        for s in range(2):
            arrived(self.buf.at[me.y, k, me.c, s], self.zr.at[k * 2 + s])
        block = self.buf.at[me.y, k, me.c]
        for way, dy in enumerate((1, -1)):
            self.sends.start(block, block, self.ys.at[way * 2 + k], self.yr.at[way * 2 + k], me.at(dy=dy))
        self.to_core(me.y, 0, k)

    def near(self, way, k):
        me, dy = self.me, (1, -1)[way]
        slot = (me.y - dy) % 4
        block = self.buf.at[slot, k, me.c]
        arrived(block, self.yr.at[way * 2 + k])
        if way == k:
            self.sends.start(block, block, self.ys.at[4 + way], self.yr.at[4 + way], me.at(dy=dy))
        self.to_core(slot, 1 + way, k)

    def far(self, k):
        slot = (self.me.y + 2) % 4
        arrived(self.buf.at[slot, k, self.me.c], self.yr.at[4 + k])
        self.to_core(slot, 3, k)

    def from_core(self):
        me = self.me
        for r, off in enumerate(OFFSETS):
            for k in range(2):
                arrived(self.buf.at[(me.y + off) % 4, k, 1 - me.c], self.cr.at[r * 2 + k])


class Scatter:
    def __init__(self, me, sends, compute, acc, bufs, sems):
        self.me, self.sends, self.compute, self.acc = me, sends, compute, acc
        self.pst, self.prv, self.fst, self.frv, self.nst, self.nrv, self.zst, self.zrv = bufs
        self.cs, self.cr, self.ys, self.yr, self.zs, self.zr = sems

    def index(self, i):
        r = 3 - i // 2
        off = jnp.where(r == 0, 0, jnp.where(r == 1, 3, jnp.where(r == 2, 1, 2)))
        return r * 2 + i % 2, (self.me.y + off) % 4, i % 2

    def to_core(self):
        me = self.me

        def step(i, _):
            s, slot, k = self.index(i)
            self.pst[s] = self.compute(slot, k, 1 - me.c).astype(BF16)
            rcopy(self.pst.at[s], self.prv.at[s], self.cs.at[s], self.cr.at[s], me.at(c=1 - me.c)).start()
            return 0

        lax.fori_loop(0, 8, step, 0)

        def finish():
            def step(s, _):
                rcopy(self.pst.at[s], self.prv.at[s], self.cs.at[s], self.cr.at[s], me.at(c=1 - me.c)).wait_send()
                return 0

            lax.fori_loop(0, 8, step, 0)

        self.sends.waits.append(finish)

    def from_core(self):
        me = self.me

        def step(i, _):
            s, slot, k = self.index(i)
            arrived(self.prv.at[s], self.cr.at[s])
            self.acc[s] = self.compute(slot, k, me.c) + self.prv[s].astype(F32)
            return 0

        lax.fori_loop(0, 8, step, 0)
        for k, dy in enumerate((1, -1)):
            self.fst[k] = self.acc[6 + k].astype(BF16)
            self.sends.start(self.fst.at[k], self.frv.at[k], self.ys.at[4 + k], self.yr.at[4 + k], me.at(dy=dy))
        for way in range(2):
            self.to_near(way, 1 - way, False)

    def to_near(self, way, k, add):
        me, dy = self.me, (1, -1)[way]
        r = 2 - way
        s = way * 2 + k
        value = self.acc[r * 2 + k]
        if add:
            arrived(self.frv.at[way], self.yr.at[4 + way])
            value = value + self.frv[way].astype(F32)
        self.nst[s] = value.astype(BF16)
        self.sends.start(self.nst.at[s], self.nrv.at[s], self.ys.at[s], self.yr.at[s], me.at(dy=dy))

    def relay(self):
        for way in range(2):
            self.to_near(way, way, True)

    def keep(self, own):
        for k in range(2):
            own[k] = self.acc[k]
        self.own = own

    def start_z(self, k):
        me = self.me
        m = self.zst.shape[1]
        total = self.own[k]
        for way in range(2):
            s = way * 2 + k
            arrived(self.nrv.at[s], self.yr.at[s])
            total = total + self.nrv[s].astype(F32)
        total = total.astype(BF16)
        for l in range(2):
            s = k * 2 + l
            self.zst[s] = total[l * m : (l + 1) * m]
            z = 4 * me.zl + s
            self.sends.start_unless_self(
                me, z, self.zst.at[s], self.zrv.at[me.zh], self.zs.at[s], self.zr.at[me.zh], me.at(z=z)
            )

    def total(self):
        value = None
        for s in range(4):
            arrived(self.zrv.at[s], self.zr.at[s])
            term = self.zrv[s].astype(F32)
            value = term if value is None else value + term
        return value


def kernel(
    text, grad_out, vision, gate, w_query, w_key, w_value, w_out, update, grad_text, grad_vision,
    wkv_g, wq_g, wo_g, text_g, grad_g, kvg_g, vis_g,
    q_acc, q_st, q_rv, att_g, dq_g, ag_acc, ag_st, ag_rv, gv_acc, gv_st, gv_rv, jg, kv_all, kvp, kvp_rv,
    probs_s, expo_acc, acc, acc_kv, own_o, own_t, own_v,
    *rest,
):
    o_bufs, t_bufs, v_bufs = rest[0:8], rest[8:16], rest[16:24]
    rest = rest[24:]
    x_sems = [rest[2 * i : 2 * i + 2] for i in range(3)]
    rest = rest[6:]
    g_sems = [rest[6 * i : 6 * i + 6] for i in range(3)]
    rest = rest[18:]
    r_sems = [rest[6 * i : 6 * i + 6] for i in range(3)]
    rest = rest[18:]
    e_ss, e_rs, m_ss, m_rs, n_ss, n_rs, l_sem = rest

    me = Here()
    sends = Sends()
    zp = me.zl + 2 * me.zh + 1 - 2 * me.zl
    piece = (me.zh % 2) * 2 + me.c

    def exchange(i, src, dst):
        sends.start(src, dst, e_ss.at[i], e_rs.at[i], me.at(z=zp))

    def mate(j):
        p = (piece + 1 + j) % 4
        return p, me.at(z=me.half * 4 + (p // 2) * 2 + me.zl, c=p % 2)

    barrier = pltpu.get_barrier_semaphore()
    around = [me.at(dx=1), me.at(dx=-1), me.at(dy=1), me.at(dy=-1), me.at(z=zp)]
    around += [mate(j)[1] for j in range(3)]
    for device in around:
        pl.semaphore_signal(barrier, inc=1, device_id=device, device_id_type=MESH)
    for i in range(4):
        for z in (me.half + 2 * i, 4 * me.zl + i):

            @pl.when(z != me.z)
            def _():
                pl.semaphore_signal(barrier, inc=1, device_id=me.at(z=z), device_id_type=MESH)

    pl.semaphore_wait(barrier, jnp.where(me.zl == me.half, 14, 16))

    gx_kv = RingGather(me, sends, wkv_g.at[me.x], wkv_g, 128, x_sems[0])
    gx_q = RingGather(me, sends, w_query, wq_g, 512, x_sems[1])
    gx_o = RingGather(me, sends, w_out, wo_g, 128, x_sems[2])
    g_text = Gather(me, sends, text, text_g, g_sems[0])
    g_grad = Gather(me, sends, grad_out, grad_g, g_sems[1])
    g_kv = Gather(me, sends, jg, kvg_g, g_sems[2])

    wkv_g[me.x, :, :HEAD] = w_key[...]
    wkv_g[me.x, :, HEAD:] = w_value[...]
    gx_kv.start()
    exchange(0, vision, vis_g.at[:, me.zl])
    g_text.start_z()
    gx_q.start()
    g_grad.start_z()
    gx_o.start()
    locals_ = [
        pltpu.make_async_copy(vision, vis_g.at[:, me.zl], l_sem.at[0]),
        pltpu.make_async_copy(w_query, wq_g.at[me.x], l_sem.at[1]),
        pltpu.make_async_copy(w_out, wo_g.at[me.x], l_sem.at[2]),
    ]
    for copy in locals_:
        copy.start()

    def kv_block(slot, k, cc):
        rows = vis_g[k * 2 + cc].reshape(128, vis_g.shape[3])
        return dot(rows, wkv_g[slot])

    gx_kv.relay(0)
    gx_kv.relay(1)
    g_text.start_y(0)
    g_text.start_y(1)
    locals_[0].wait()
    arrived(vis_g.at[:, 1 - me.zl], e_rs.at[0])
    gx_kv.finish()
    s_kv = Scatter(me, sends, kv_block, acc_kv, v_bufs, r_sems[2])
    s_kv.to_core()
    s_kv.from_core()
    s_kv.keep(own_v)
    gx_q.relay(0)
    gx_q.relay(1)
    s_kv.relay()
    g_text.near(0, 0)
    g_text.near(1, 1)
    g_text.near(0, 1)
    g_text.near(1, 0)
    gx_o.relay(0)
    gx_o.relay(1)
    g_grad.start_y(0)
    g_grad.start_y(1)
    s_kv.start_z(0)
    s_kv.start_z(1)
    g_text.far(0)
    g_text.far(1)

    projected = s_kv.total()
    keys = projected[:, :HEAD]
    key_scale = lax.rsqrt(jnp.mean(keys * keys, axis=-1, keepdims=True) + EPS)
    kv_all[piece, :, :HEAD] = (keys * key_scale).astype(BF16)
    kv_all[piece, :, HEAD:] = projected[:, HEAD:].astype(BF16)
    own_v[0, :64] = projected
    for j in range(3):
        p, device = mate(j)
        sends.start(kv_all.at[piece], kv_all.at[piece], m_ss.at[j], m_rs.at[piece], device)

    g_text.from_core()
    gx_q.finish()
    locals_[1].wait()
    q_acc[...] = jnp.zeros_like(q_acc)

    def q_step(i, _):
        rows = text_g[i // 4, (i % 4) // 2, i % 2].reshape(512, 256)
        block = wq_g[i // 4, pl.ds(pl.multiple_of((i % 4) * 256, 256), 256), :]
        q_acc[...] += dot(rows, block).reshape(2, 256, 256)
        return 0

    lax.fori_loop(0, 16, q_step, 0)
    q_st[...] = q_acc[1 - me.zl].astype(BF16)
    exchange(1, q_st, q_rv)

    g_grad.near(0, 0)
    g_grad.near(1, 1)
    g_grad.near(0, 1)
    g_grad.near(1, 0)

    for j in range(3):
        p, _ = mate(j)
        arrived(kv_all.at[p], m_rs.at[p])
    kv = kv_all[...].reshape(256, 256)
    key_head, value_head = kv[:, :HEAD], kv[:, HEAD:]
    scale = HEAD ** (-0.5)
    tanh_gate = jnp.tanh(gate[...])

    arrived(q_rv, e_rs.at[1])
    query = q_acc[me.zl] + q_rv[...].astype(F32)
    q_acc[0] = query
    for h in range(2):
        q = query[:, h * HEAD : (h + 1) * HEAD]
        q_scale = lax.rsqrt(jnp.mean(q * q, axis=-1, keepdims=True) + EPS)
        q_normed = (q * q_scale).astype(BF16)
        expo = jnp.exp(dot(q_normed, key_head, NT) * scale)
        probs = expo / jnp.sum(expo, axis=-1, keepdims=True)
        expo_acc[h] = probs
        low = probs.astype(BF16)
        probs_s[h] = low
        att_g[me.zl, :, h * HEAD : (h + 1) * HEAD] = dot(low, value_head).astype(BF16)
    exchange(2, att_g.at[me.zl], att_g.at[me.zl])
    g_grad.far(0)
    g_grad.far(1)

    gx_o.finish()
    locals_[2].wait()

    def out_block(slot, k, cc):
        block = wo_g[slot, :, pl.ds(pl.multiple_of((k * 2 + cc) * 256, 256), 256)]
        return dot(att_g[...].reshape(512, 256), block)

    arrived(att_g.at[1 - me.zl], e_rs.at[2])
    s_out = Scatter(me, sends, out_block, acc, o_bufs, r_sems[0])
    s_out.to_core()
    s_out.from_core()
    s_out.keep(own_o)

    g_grad.from_core()
    ag_acc[...] = jnp.zeros_like(ag_acc)

    def ag_step(i, _):
        rows = grad_g[i // 4, (i % 4) // 2, i % 2].reshape(512, 256)
        block = wo_g[i // 4, :, pl.ds(pl.multiple_of((i % 4) * 256, 256), 256)]
        ag_acc[...] += dot(rows, block, NT).reshape(2, 256, 256)
        return 0

    lax.fori_loop(0, 16, ag_step, 0)
    ag_st[...] = ag_acc[1 - me.zl].astype(BF16)
    exchange(3, ag_st, ag_rv)
    s_out.relay()
    arrived(ag_rv, e_rs.at[3])
    attend_grad = (tanh_gate * (ag_acc[me.zl] + ag_rv[...].astype(F32))).astype(BF16)
    key_part = jnp.zeros((256, HEAD), F32)
    value_part = jnp.zeros((256, HEAD), F32)
    for h in range(2):
        q = q_acc[0, :, h * HEAD : (h + 1) * HEAD]
        q_scale = lax.rsqrt(jnp.mean(q * q, axis=-1, keepdims=True) + EPS)
        q_normed = (q * q_scale).astype(BF16)
        a_grad = attend_grad[:, h * HEAD : (h + 1) * HEAD]
        probs = expo_acc[h]
        prob_grad = dot(a_grad, value_head, NT)
        delta = jnp.sum(probs * prob_grad, axis=-1, keepdims=True)
        score_grad = (probs * (prob_grad - delta) * scale).astype(BF16)
        normed_grad = dot(score_grad, key_head)
        mean = jnp.mean(normed_grad * q, axis=-1, keepdims=True)
        q_grad = q_scale * normed_grad - q * (q_scale * q_scale * q_scale) * mean
        dq_g[me.zl, :, h * HEAD : (h + 1) * HEAD] = q_grad.astype(BF16)
        key_part = key_part + dot(score_grad, q_normed, TN)
        value_part = value_part + dot(probs_s[h], a_grad, TN)
    exchange(4, dq_g.at[me.zl], dq_g.at[me.zl])
    kvp[:, :, :HEAD] = key_part.astype(BF16).reshape(4, 64, HEAD)
    kvp[:, :, HEAD:] = value_part.astype(BF16).reshape(4, 64, HEAD)
    for j in range(3):
        p, device = mate(j)
        sends.start(kvp.at[p], kvp_rv.at[piece], n_ss.at[j], n_rs.at[piece], device)

    kv_grad = kvp[piece].astype(F32)
    for j in range(3):
        p, _ = mate(j)
        arrived(kvp_rv.at[p], n_rs.at[p])
        kv_grad = kv_grad + kvp_rv[p].astype(F32)
    keys = own_v[0, :64, :HEAD]
    key_scale = lax.rsqrt(jnp.mean(keys * keys, axis=-1, keepdims=True) + EPS)
    k_grad = kv_grad[:, :HEAD]
    mean = jnp.mean(k_grad * keys, axis=-1, keepdims=True)
    k_grad = key_scale * k_grad - keys * (key_scale * key_scale * key_scale) * mean
    jg[:, :HEAD] = k_grad.astype(BF16)
    jg[:, HEAD:] = kv_grad[:, HEAD:].astype(BF16)
    g_kv.start_z()

    def text_block(slot, k, cc):
        block = wq_g[slot, pl.ds(pl.multiple_of((k * 2 + cc) * 256, 256), 256), :]
        return dot(dq_g[...].reshape(512, 256), block, NT)

    arrived(dq_g.at[1 - me.zl], e_rs.at[4])
    s_text = Scatter(me, sends, text_block, acc, t_bufs, r_sems[1])
    s_text.to_core()
    s_text.from_core()
    s_text.keep(own_t)
    s_out.start_z(0)
    s_out.start_z(1)
    g_kv.start_y(0)
    g_kv.start_y(1)
    s_text.relay()
    g_kv.near(0, 0)
    g_kv.near(1, 1)
    g_kv.near(0, 1)
    g_kv.near(1, 0)
    update[...] = (tanh_gate * s_out.total()).astype(BF16)
    g_kv.far(0)
    g_kv.far(1)
    g_kv.from_core()

    gv_acc[...] = jnp.zeros_like(gv_acc)

    def gv_step(i, _):
        rows = kvg_g[i].reshape(512, 256)
        gv_acc[...] += dot(rows, wkv_g[i], NT).reshape(4, 2, 64, -1)
        return 0

    lax.fori_loop(0, 4, gv_step, 0)
    gv_st[...] = gv_acc[:, 1 - me.zl].astype(BF16)
    exchange(5, gv_st, gv_rv)
    s_text.start_z(0)
    s_text.start_z(1)
    arrived(gv_rv, e_rs.at[5])
    grad_vision[...] = (gv_acc[:, me.zl] + gv_rv[...].astype(F32)).astype(BF16)
    grad_text[...] = s_text.total().astype(BF16)
    sends.finish()


def body(text, grad_out, vision, gate, w_query, w_key, w_value, w_out):
    features = vision.shape[1]
    dma = lambda n: pltpu.SemaphoreType.DMA((n,))
    vm = pltpu.VMEM

    def scatter_bufs(m):
        return [
            vm((8, 2 * m, 256), BF16), vm((8, 2 * m, 256), BF16),
            vm((2, 2 * m, 256), BF16), vm((2, 2 * m, 256), BF16),
            vm((4, 2 * m, 256), BF16), vm((4, 2 * m, 256), BF16),
            vm((4, m, 256), BF16), vm((4, m, 256), BF16),
        ]

    scratch = [
        vm((4, features, 256), BF16), vm((4, 1024, 256), BF16), vm((4, 256, 1024), BF16),
        vm((4, 2, 2, 2, 256, 256), BF16), vm((4, 2, 2, 2, 256, 256), BF16), vm((4, 2, 2, 2, 64, 256), BF16),
        vm((4, 2, 64, features), BF16),
        vm((2, 256, 256), F32), vm((256, 256), BF16), vm((256, 256), BF16),
        vm((2, 256, 256), BF16), vm((2, 256, 256), BF16),
        vm((2, 256, 256), F32), vm((256, 256), BF16), vm((256, 256), BF16),
        vm((4, 2, 64, features), F32), vm((4, 64, features), BF16), vm((4, 64, features), BF16),
        vm((64, 256), BF16), vm((4, 64, 256), BF16), vm((4, 64, 256), BF16), vm((4, 64, 256), BF16),
        vm((2, 256, 256), BF16), vm((2, 256, 256), F32),
        vm((8, 512, 256), F32), vm((8, 128, 256), F32),
        vm((2, 512, 256), F32), vm((2, 512, 256), F32), vm((2, 128, 256), F32),
    ]
    scratch += scatter_bufs(256) + scatter_bufs(256) + scatter_bufs(64)
    scratch += [dma(4), dma(4)] * 3
    scratch += [dma(4), dma(4), dma(6), dma(6), dma(8), dma(8)] * 3
    scratch += [dma(8), dma(8), dma(6), dma(6), dma(4), dma(4)] * 3
    scratch += [dma(6), dma(6), dma(3), dma(4), dma(3), dma(4), dma(3)]
    whole = pl.BlockSpec(memory_space=pltpu.VMEM)
    update, grad_text, grad_vision = pl.pallas_call(
        kernel,
        out_shape=(
            jax.ShapeDtypeStruct((256, 256), BF16),
            jax.ShapeDtypeStruct((256, 256), BF16),
            jax.ShapeDtypeStruct((4, 64, features), BF16),
        ),
        in_specs=[whole] * 8,
        out_specs=(whole,) * 3,
        scratch_shapes=scratch,
        name="cross_attention",
        compiler_params=pltpu.CompilerParams(
            collective_id=0, has_side_effects=True, vmem_limit_bytes=60 * 2**20
        ),
    )(
        text, grad_out, vision.reshape(4, 64, features), gate.reshape(1, 1),
        w_query, w_key, w_value, w_out,
    )
    return update, grad_text, grad_vision.reshape(256, features)


def solution(mesh):
    return jax.shard_map(
        body,
        mesh=mesh,
        in_specs=(
            P("dp", "tensor"), P("dp", "tensor"), P("dp", "tensor"), P(),
            P("dp", "tensor"), P("tensor", "dp"), P("tensor", "dp"), P("tensor", "dp"),
        ),
        out_specs=(P("dp", "tensor"), P("dp", "tensor"), P("dp", "tensor")),
        check_vma=False,
    )
```

```python
import jax
import jax.numpy as jnp
from jax import lax
from jax.experimental import pallas as pl
from jax.experimental.pallas import tpu as pltpu
from jax.sharding import PartitionSpec as P

HEAD = 128
EPS = 1e-05
MESH = pl.DeviceIdType.MESH
F32 = jnp.float32
BF16 = jnp.bfloat16
OFFSETS = (0, 3, 1, 2)
NT = (((1,), (1,)), ((), ()))
TN = (((0,), (0,)), ((), ()))


def dot(a, b, dims=(((1,), (0,)), ((), ()))):
    return lax.dot_general(a, b, dims, preferred_element_type=F32)


class Here:
    def __init__(self):
        d, t = lax.axis_index("dp"), lax.axis_index("tensor")
        self.x, self.zl = d // 2, d % 2
        self.y, self.zh, self.c = t // 8, (t // 2) % 4, t % 2
        self.z = 2 * self.zh + self.zl
        self.half = self.zh // 2
        self.kept = self.zl == self.half
        self.place = jnp.where(self.zl == 0, self.z, 7 - self.z) // 2
        self.next_z = (self.z + jnp.where(self.place == 2, 2, -2) * (1 - 2 * self.zl)) % 8
        self.toward = 1 - 2 * self.half

    def order(self, i):
        u = self.place
        table = ((0, 1, 2, 3), (2, 1, 3, 0), (3, 2, 0, 1), (0, 1, 2, 3))
        j = table[3][i]
        for n in (2, 1, 0):
            j = jnp.where(u == n, table[n][i], j)
        return jnp.where(self.zl == 0, j, 3 - j)

    def at(self, dx=0, dy=0, z=None, c=None):
        x = (self.x + dx) % 4 if dx else self.x
        y = (self.y + dy) % 4 if dy else self.y
        z = self.z if z is None else z
        c = self.c if c is None else c
        return (x * 2 + z % 2, y * 8 + (z // 2) * 2 + c)


def rcopy(src, dst, send, recv, device):
    return pltpu.make_async_remote_copy(
        src_ref=src, dst_ref=dst, send_sem=send, recv_sem=recv, device_id=device, device_id_type=MESH
    )


class Sends:
    def __init__(self):
        self.waits = []

    def start(self, *args):
        copy = rcopy(*args)
        copy.start()
        self.waits.append(copy.wait_send)

    def start_unless_self(self, me, z, src, dst, send, recv, device):
        @pl.when(z != me.z)
        def _():
            rcopy(src, dst, send, recv, device).start()

        @pl.when(z == me.z)
        def _():
            pltpu.make_async_copy(src, dst, recv).start()

        def finish():
            @pl.when(z != me.z)
            def _():
                rcopy(src, dst, send, recv, device).wait_send()

        self.waits.append(finish)

    def finish(self):
        for wait in self.waits:
            wait()


def arrived(dst, sem):
    pltpu.make_async_copy(dst, dst, sem).wait()


class RingGather:
    def __init__(self, me, sends, own, buf, cut, sems):
        self.me, self.sends, self.own, self.buf, self.cut = me, sends, own, buf, cut
        self.ss, self.rs = sems

    def start(self):
        me = self.me
        for way, dx in enumerate((1, -1)):
            self.sends.start(self.own, self.buf.at[me.x], self.ss.at[way], self.rs.at[way], me.at(dx=dx))

    def part(self, slot, way):
        rows = self.buf.shape[1]
        lo, n = ((0, self.cut), (self.cut, rows - self.cut))[way]
        return self.buf.at[slot, pl.ds(lo, n)]

    def relay(self, way):
        me, dx = self.me, (1, -1)[way]
        slot = (me.x - dx) % 4
        arrived(self.buf.at[slot], self.rs.at[way])
        block = self.part(slot, way)
        self.sends.start(block, block, self.ss.at[2 + way], self.rs.at[2 + way], me.at(dx=dx))

    def finish(self):
        for way in range(2):
            arrived(self.part((self.me.x + 2) % 4, way), self.rs.at[2 + way])


class Gather:
    def __init__(self, me, sends, own, buf, sems):
        self.me, self.sends, self.own, self.buf = me, sends, own, buf
        self.zs, self.zr, self.ys, self.yr, self.cs, self.cr = sems

    def start_z(self, later=False):
        me = self.me
        dst = self.buf.at[me.y, me.zh % 2, me.c, me.zl]
        recv = self.zr.at[(me.zh % 2) * 2 + me.zl]
        one = me.toward * jnp.where(me.kept, -2, 1)
        args = [
            (self.own, dst, self.zs.at[i], recv, me.at(z=(me.z + sign * one) % 8)) for i, sign in enumerate((1, -1))
        ]
        self.sends.start(*args[0])
        self.sends.waits.append(rcopy(*args[1]).wait_send)

        def second():
            rcopy(*args[1]).start()

        @pl.when(me.kept)
        def _():
            pltpu.make_async_copy(self.own, dst, recv).start()

        if not later:
            second()
            return None

        pl.when(jnp.logical_not(me.kept))(second)
        return lambda: pl.when(me.kept)(second)

    def relay_z(self, i):
        if i == 3:
            return
        me = self.me
        cond = (me.place >= 2, me.place != 1, me.place == 1)[i]
        block, sem = self.block(me.y, i), self.zs.at[2 + i % 2]
        args = block, block, sem, self.zr.at[me.order(i)], me.at(z=me.next_z)

        @pl.when(cond)
        def _():
            rcopy(*args).start()

        def finish():
            @pl.when(cond)
            def _():
                rcopy(*args).wait_send()

        self.sends.waits.append(finish)

    def block(self, slot, i):
        j = self.me.order(i)
        return self.buf.at[slot, j // 2, self.me.c, j % 2]

    def to_core(self, slot, r, i):
        block = self.block(slot, i)
        rcopy(block, block, self.cs.at[0], self.cr.at[r], self.me.at(c=1 - self.me.c)).start()

    def arrive(self, *positions):
        for i in positions:
            arrived(self.block(self.me.y, i), self.zr.at[self.me.order(i)])
            self.relay_z(i)

    def start_y(self, *positions):
        me = self.me
        for i in positions:
            block = self.block(me.y, i)
            for way, dy in enumerate((1, -1)):
                rcopy(block, block, self.ys.at[way], self.yr.at[way * 4 + i], me.at(dy=dy)).start()
            self.to_core(me.y, 0, i)

    def near(self, *positions):
        me = self.me
        for i in positions:
            for way, dy in enumerate((1, -1)):
                slot = (me.y - dy) % 4
                block = self.block(slot, i)
                arrived(block, self.yr.at[way * 4 + i])
                if way == i % 2:
                    rcopy(block, block, self.ys.at[2 + way], self.yr.at[8 + i], me.at(dy=dy)).start()
                self.to_core(slot, 1 + way, i)

    def far(self, *positions):
        slot = (self.me.y + 2) % 4
        for i in positions:
            arrived(self.block(slot, i), self.yr.at[8 + i])
            self.to_core(slot, 3, i)

    def from_core(self, *rs):
        me = self.me
        for r in rs:
            arrived(self.buf.at[(me.y + OFFSETS[r]) % 4, :, 1 - me.c], self.cr.at[r])
        if 3 in rs:
            self.sends.waits.append(self.sent)

    def sent(self):
        c = self.me.c
        arrived(self.buf.at[:, :, c], self.cs.at[0])
        for way in range(2):
            arrived(self.buf.at[0, :, c], self.ys.at[way])
            arrived(self.buf.at[0, 0, c], self.ys.at[2 + way])


class Scatter:
    def __init__(self, me, sends, compute, acc, bufs, sems):
        self.me, self.sends, self.compute, self.acc = me, sends, compute, acc
        self.pst, self.prv, self.fst, self.frv, self.nst, self.nrv, self.zst, self.zrv = bufs
        self.cs, self.cr, self.ys, self.yr, self.zs, self.zr = sems

    def to_core(self, *rs):
        me = self.me
        for r in rs:

            def step(k, _):
                s = r * 2 + k
                self.pst[s] = self.compute((me.y + OFFSETS[r]) % 4, k, 1 - me.c).astype(BF16)
                rcopy(self.pst.at[s], self.prv.at[s], self.cs.at[0], self.cr.at[r], me.at(c=1 - me.c)).start()
                return 0

            lax.fori_loop(0, 2, step, 0)

    def from_core(self, r):
        me = self.me
        arrived(self.prv.at[pl.ds(r * 2, 2)], self.cr.at[r])

        def step(k, _):
            s = r * 2 + k
            value = self.compute((me.y + OFFSETS[r]) % 4, k, me.c) + self.prv[s].astype(F32)
            self.acc[s] = value.reshape(self.acc.shape[1:])
            return 0

        lax.fori_loop(0, 2, step, 0)

    def mine(self, r, i):
        j = self.me.order(3 - i)
        return self.acc[r * 2 + j // 2, j % 2]

    def send_far(self):
        me = self.me
        self.from_core(3)
        for i in range(4):
            self.fst[i] = self.mine(3, i).astype(BF16)
            self.sends.start(
                self.fst.at[i], self.frv.at[i], self.ys.at[8 + i], self.yr.at[8 + i], me.at(dy=(1, -1)[i % 2])
            )

    def begin(self):
        self.to_core(3)
        self.to_core(2, 1)
        self.send_far()
        self.from_core(2)
        self.near((0, 1))
        self.from_core(1)
        self.near((1, 0))
        self.to_core(0)
        self.sends.waits.append(lambda: arrived(self.pst, self.cs.at[0]))

    def near(self, *items):
        me = self.me
        for way, i in items:
            s = way * 4 + i
            value = self.mine(2 - way, i)
            if i % 2 == way:
                arrived(self.frv.at[i], self.yr.at[8 + i])
                value = value + self.frv[i].astype(F32)
            self.nst[s] = value.astype(BF16)
            self.sends.start(self.nst.at[s], self.nrv.at[s], self.ys.at[s], self.yr.at[s], me.at(dy=(1, -1)[way]))

    def start_z(self, *positions):
        me = self.me
        for i in positions:
            total = self.mine(0, i)
            for way in range(2):
                s = way * 4 + i
                arrived(self.nrv.at[s], self.yr.at[s])
                total = total + self.nrv[s].astype(F32)
            self.zst[i] = total.astype(BF16)
            z = 4 * me.zl + me.order(3 - i)
            self.sends.start_unless_self(
                me, z, self.zst.at[i], self.zrv.at[me.zh], self.zs.at[i], self.zr.at[me.zh], me.at(z=z)
            )

    def total(self):
        value = None
        for s in range(4):
            arrived(self.zrv.at[s], self.zr.at[s])
            term = self.zrv[s].astype(F32)
            value = term if value is None else value + term
        return value


def kernel(
    text, grad_out, vision, gate, w_query, w_key, w_value, w_out, update, grad_text, grad_vision,
    wkv_g, wq_g, wo_g, text_g, grad_g, kvg_g, vis_g, vis_r,
    q_acc, q_st, q_rv, att_g, dq_g, ag_acc, ag_st, ag_rv, gv_acc, gv_st, gv_rv, jg, kv_all, kvp, kvp_rv,
    probs_low, probs, query, query_low, query_scale, attend_grad, score_grad, acc_o, acc_t, acc_v, own_kv,
    *rest,
):
    o_bufs, t_bufs, v_bufs = rest[0:8], rest[8:16], rest[16:24]
    rest = rest[24:]
    x_sems = [rest[2 * i : 2 * i + 2] for i in range(3)]
    rest = rest[6:]
    g_sems = [rest[6 * i : 6 * i + 6] for i in range(3)]
    rest = rest[18:]
    r_sems = [rest[6 * i : 6 * i + 6] for i in range(3)]
    rest = rest[18:]
    e_ss, e_rs, m_ss, m_rs, n_ss, n_rs, l_sem = rest

    me = Here()
    sends = Sends()
    zp = me.zl + 2 * me.zh + 1 - 2 * me.zl
    piece = (me.zh % 2) * 2 + me.c
    near_y = [(me.y + off) % 4 for off in OFFSETS]

    def exchange(i, src, dst):
        sends.start(src, dst, e_ss.at[i], e_rs.at[i], me.at(z=zp))

    def mate(j):
        p = (piece + 1 + j) % 4
        return p, me.at(z=me.half * 4 + (p // 2) * 2 + me.zl, c=p % 2)

    gx_kv = RingGather(me, sends, wkv_g.at[me.x], wkv_g, 128, x_sems[0])
    gx_q = RingGather(me, sends, w_query, wq_g, 512, x_sems[1])
    gx_o = RingGather(me, sends, w_out, wo_g, 128, x_sems[2])
    g_text = Gather(me, sends, text, text_g, g_sems[0])
    g_grad = Gather(me, sends, grad_out, grad_g, g_sems[1])
    g_kv = Gather(me, sends, jg, kvg_g, g_sems[2])

    barrier = pltpu.get_barrier_semaphore()
    around = [me.at(dx=1), me.at(dx=-1), me.at(dy=1), me.at(dy=-1), me.at(z=zp)]
    around += [mate(j)[1] for j in range(3)]
    for device in around:
        pl.semaphore_signal(barrier, inc=1, device_id=device, device_id_type=MESH)
    for i in range(4):
        for z in (me.half + 2 * i, 4 * me.zl + i):

            @pl.when(z != me.z)
            def _():
                pl.semaphore_signal(barrier, inc=1, device_id=me.at(z=z), device_id_type=MESH)

    @pl.when(jnp.logical_not(me.kept))
    def _():
        pl.semaphore_signal(barrier, inc=1, device_id=me.at(z=me.next_z), device_id_type=MESH)

    local_q = pltpu.make_async_copy(w_query, wq_g.at[me.x], l_sem.at[0])
    local_o = pltpu.make_async_copy(w_out, wo_g.at[me.x], l_sem.at[1])
    local_q.start()
    local_o.start()
    wkv_g[me.x, :, :HEAD] = w_key[...]
    wkv_g[me.x, :, HEAD:] = w_value[...]
    pl.semaphore_wait(barrier, jnp.where(me.kept, 14, 17))

    second = g_text.start_z(later=True)
    gx_kv.start()
    exchange(0, vision, vis_g)

    def kv_block(slot, k, cc):
        return dot(vis_r[k * 2 + cc].reshape(128, vis_r.shape[3]), wkv_g[slot])

    @pl.when(me.kept)
    def _():
        arrived(g_text.block(me.y, 0), g_text.zr.at[me.order(0)])
        g_text.start_y(0)

    vis_r[:, me.zl] = vision[...].T.reshape(4, 64, -1)
    gx_kv.relay(0)
    gx_kv.relay(1)
    gx_q.start()
    second()

    @pl.when(jnp.logical_not(me.kept))
    def _():
        arrived(g_text.block(me.y, 0), g_text.zr.at[me.order(0)])
        g_text.start_y(0)

    g_text.relay_z(0)
    g_text.arrive(1)
    g_text.start_y(1)
    g_text.near(0)
    g_text.arrive(2)
    g_text.start_y(2)
    with jax.named_scope("vis_wait"):
        arrived(vis_g, e_rs.at[0])
    vis_r[:, 1 - me.zl] = vis_g[...].T.reshape(4, 64, -1)
    gx_kv.finish()
    s_kv = Scatter(me, sends, kv_block, acc_v, v_bufs, r_sems[2])
    s_kv.to_core(3, 2, 1, 0)
    g_text.arrive(3)
    g_text.start_y(3)
    g_grad.start_z()
    s_kv.send_far()
    g_text.near(1)
    s_kv.from_core(2)
    s_kv.from_core(1)
    s_kv.near((0, 1), (1, 0), (0, 3), (1, 2))
    s_kv.from_core(0)
    sends.waits.append(lambda: arrived(s_kv.pst, s_kv.cs.at[0]))
    g_text.near(2)
    gx_q.relay(0)
    gx_q.relay(1)
    gx_o.start()
    s_kv.near((0, 0), (1, 1), (0, 2), (1, 3))
    g_grad.arrive(0)
    g_text.near(3)
    g_grad.arrive(1)
    g_grad.start_y(0, 1)
    s_kv.start_z(0, 1, 2, 3)

    def q_part(slot):
        total = None
        for j in range(4):
            term = dot(text_g[slot, j // 2, j % 2].reshape(512, 256), wq_g[slot, pl.ds(j * 256, 256), :])
            total = term if total is None else total + term
        return total.reshape(2, 256, 256)

    g_text.far(0, 1, 2, 3)
    g_grad.arrive(2)
    g_grad.start_y(2)
    g_text.from_core(0, 1, 2)
    local_q.wait()
    gx_q.finish()
    with jax.named_scope("query"):
        q_acc[...] = q_part(near_y[0])
        q_acc[...] += q_part(near_y[1])
        q_acc[...] += q_part(near_y[2])
    g_text.from_core(3)
    with jax.named_scope("query_last"):
        q_acc[...] += q_part(near_y[3])
        for h in range(2):
            q_st[h] = q_acc[1 - me.zl, :, h * HEAD : (h + 1) * HEAD].astype(BF16)
            exchange(1 + h, q_st.at[h], q_rv.at[h])
    g_grad.arrive(3)
    g_grad.start_y(3)

    with jax.named_scope("kv"):
        projected = s_kv.total()
        keys = projected[:, :HEAD]
        key_scale = lax.rsqrt(jnp.mean(keys * keys, axis=-1, keepdims=True) + EPS)
        kv_all[piece, :, :HEAD] = (keys * key_scale).astype(BF16)
        kv_all[piece, :, HEAD:] = projected[:, HEAD:].astype(BF16)
        own_kv[...] = projected
        for j in range(3):
            p, device = mate(j)
            sends.start(kv_all.at[piece], kv_all.at[piece], m_ss.at[j], m_rs.at[piece], device)

    g_grad.near(0)
    with jax.named_scope("kv_wait"):
        for j in range(3):
            p, _ = mate(j)
            arrived(kv_all.at[p], m_rs.at[p])
    kv = kv_all[...].reshape(256, 256)
    key_head, value_head = kv[:, :HEAD], kv[:, HEAD:]
    scale = HEAD ** (-0.5)
    tanh_gate = jnp.tanh(gate[...])

    for h in range(2):
        own = slice(h * HEAD, (h + 1) * HEAD)
        with jax.named_scope("q_wait"):
            arrived(q_rv.at[h], e_rs.at[1 + h])
        with jax.named_scope("attention"):
            q = q_acc[me.zl, :, own] + q_rv[h].astype(F32)
            q_scale = lax.rsqrt(jnp.mean(q * q, axis=-1, keepdims=True) + EPS)
            q_normed = (q * q_scale).astype(BF16)
            query[h] = q
            query_low[h] = q_normed
            query_scale[h] = jnp.broadcast_to(q_scale, q.shape)
            expo = jnp.exp(dot(q_normed, key_head, NT) * scale)
            prob = expo / jnp.sum(expo, axis=-1, keepdims=True)
            probs[h] = prob
            low = prob.astype(BF16)
            probs_low[h] = low
            att_g[me.zl, :, own] = dot(low, value_head).astype(BF16)
            exchange(3 + h, att_g.at[me.zl, :, own], att_g.at[me.zl, :, own])
    g_grad.near(1, 2)
    gx_o.relay(0)
    gx_o.relay(1)
    g_grad.near(3)

    def ag_part(slot):
        total = None
        for j in range(4):
            term = dot(grad_g[slot, j // 2, j % 2].reshape(512, 256), wo_g[slot, :, pl.ds(j * 256, 256)], NT)
            total = term if total is None else total + term
        return total.reshape(2, 256, 256)

    def out_block(slot, k, cc):
        block = wo_g[slot, :, pl.ds(pl.multiple_of((k * 2 + cc) * 256, 256), 256)]
        return dot(att_g[...].reshape(512, 256), block)

    with jax.named_scope("att_wait"):
        for h in range(2):
            theirs = att_g.at[1 - me.zl, :, pl.ds(h * HEAD, HEAD)]
            arrived(theirs, e_rs.at[3 + h])
    s_out = Scatter(me, sends, out_block, acc_o, o_bufs, r_sems[0])
    g_grad.far(0, 1)
    local_o.wait()
    gx_o.finish()
    s_out.begin()
    s_out.near((0, 3), (1, 2))

    g_grad.far(2, 3)
    g_grad.from_core(0, 1, 2)
    with jax.named_scope("attend_grad"):
        ag_acc[...] = ag_part(near_y[0])
        ag_acc[...] += ag_part(near_y[1])
        ag_acc[...] += ag_part(near_y[2])
    g_grad.from_core(3)
    with jax.named_scope("attend_grad_last"):
        ag_acc[...] += ag_part(near_y[3])
        for h in range(2):
            ag_st[h] = ag_acc[1 - me.zl, :, h * HEAD : (h + 1) * HEAD].astype(BF16)
            exchange(5 + h, ag_st.at[h], ag_rv.at[h])
    s_out.from_core(0)
    s_out.near((0, 0), (1, 1))

    for h in range(2):
        own = slice(h * HEAD, (h + 1) * HEAD)
        with jax.named_scope("ag_wait"):
            arrived(ag_rv.at[h], e_rs.at[5 + h])
        with jax.named_scope("backward"):
            a_grad = (tanh_gate * (ag_acc[me.zl, :, own] + ag_rv[h].astype(F32))).astype(BF16)
            attend_grad[h] = a_grad
            prob = probs[h]
            prob_grad = dot(a_grad, value_head, NT)
            delta = jnp.sum(prob * prob_grad, axis=-1, keepdims=True)
            s_grad = (prob * (prob_grad - delta) * scale).astype(BF16)
            score_grad[h] = s_grad
            normed_grad = dot(s_grad, key_head)
            q, q_scale = query[h], query_scale[h]
            mean = jnp.mean(normed_grad * q, axis=-1, keepdims=True)
            q_grad = q_scale * (normed_grad - q * (q_scale * q_scale) * mean)
            dq_g[me.zl, :, own] = q_grad.astype(BF16)
        if h == 0:
            exchange(7, dq_g.at[me.zl, :, own], dq_g.at[me.zl, :, own])
            s_out.near((0, 2), (1, 3))
    with jax.named_scope("kv_part"):
        key_part = dot(score_grad[0], query_low[0], TN) + dot(score_grad[1], query_low[1], TN)
        value_part = dot(probs_low[0], attend_grad[0], TN) + dot(probs_low[1], attend_grad[1], TN)
        kvp[:, :, :HEAD] = key_part.astype(BF16).reshape(4, 64, HEAD)
        kvp[:, :, HEAD:] = value_part.astype(BF16).reshape(4, 64, HEAD)
        for j in range(3):
            p, device = mate(j)
            sends.start(kvp.at[p], kvp_rv.at[piece], n_ss.at[j], n_rs.at[piece], device)
    exchange(8, dq_g.at[me.zl, :, HEAD:], dq_g.at[me.zl, :, HEAD:])

    with jax.named_scope("kv_grad"):
        kv_grad = kvp[piece].astype(F32)
        for j in range(3):
            p, _ = mate(j)
            arrived(kvp_rv.at[p], n_rs.at[p])
            kv_grad = kv_grad + kvp_rv[p].astype(F32)
        keys = own_kv[:, :HEAD]
        key_scale = lax.rsqrt(jnp.mean(keys * keys, axis=-1, keepdims=True) + EPS)
        k_grad = kv_grad[:, :HEAD]
        mean = jnp.mean(k_grad * keys, axis=-1, keepdims=True)
        k_grad = key_scale * k_grad - keys * (key_scale * key_scale * key_scale) * mean
        jg[:, :HEAD] = k_grad.astype(BF16)
        jg[:, HEAD:] = kv_grad[:, HEAD:].astype(BF16)
        g_kv.start_z()

    def text_block(slot, k, cc):
        block = wq_g[slot, pl.ds(pl.multiple_of((k * 2 + cc) * 256, 256), 256), :]
        return dot(dq_g[...].reshape(512, 256), block, NT)

    with jax.named_scope("dq_wait"):
        for h in range(2):
            theirs = dq_g.at[1 - me.zl, :, pl.ds(h * HEAD, HEAD)]
            arrived(theirs, e_rs.at[7 + h])
    s_text = Scatter(me, sends, text_block, acc_t, t_bufs, r_sems[1])
    s_text.to_core(3)
    s_text.to_core(2, 1)
    s_text.send_far()
    g_kv.arrive(0, 1)
    s_text.from_core(2)
    s_text.near((0, 1))
    s_text.from_core(1)
    s_text.near((1, 0))
    s_text.to_core(0)
    sends.waits.append(lambda: arrived(s_text.pst, s_text.cs.at[0]))
    g_kv.arrive(2, 3)
    g_kv.start_y(0, 1, 2, 3)
    s_text.from_core(0)
    s_out.start_z(0, 1, 2, 3)
    s_text.near((0, 0), (1, 1))
    g_kv.near(0, 1, 2, 3)
    s_text.near((0, 2), (1, 2), (0, 3), (1, 3))
    s_text.start_z(0)
    g_kv.far(0, 1, 2, 3)
    g_kv.from_core(0, 1, 2, 3)

    with jax.named_scope("vision_grad"):
        gv = None
        for i in range(4):
            term = dot(kvg_g[i].reshape(512, 256), wkv_g[i], NT)
            gv = term if gv is None else gv + term
        gv_acc[...] = gv.reshape(4, 2, 64, -1)
        gv_st[...] = gv_acc[:, 1 - me.zl].astype(BF16)
        exchange(9, gv_st, gv_rv)
    s_text.start_z(1, 2, 3)
    with jax.named_scope("vision_grad_last"):
        arrived(gv_rv, e_rs.at[9])
        total = gv_acc[:, me.zl] + gv_rv[...].astype(F32)
        grad_vision[...] = total.reshape(256, -1).T.astype(BF16)
    with jax.named_scope("update"):
        update[...] = (tanh_gate * s_out.total()).astype(BF16)
    with jax.named_scope("text_grad_last"):
        grad_text[...] = s_text.total().astype(BF16)
    with jax.named_scope("sends"):
        sends.finish()


def body(text, grad_out, vision, gate, w_query, w_key, w_value, w_out):
    features = vision.shape[1]
    dma = lambda n: pltpu.SemaphoreType.DMA((n,))
    vm = pltpu.VMEM

    def scatter_bufs(m):
        return [
            vm((8, 2 * m, 256), BF16), vm((8, 2 * m, 256), BF16),
            vm((4, m, 256), BF16), vm((4, m, 256), BF16),
            vm((8, m, 256), BF16), vm((8, m, 256), BF16),
            vm((4, m, 256), BF16), vm((4, m, 256), BF16),
        ]

    scratch = [
        vm((4, features, 256), BF16), vm((4, 1024, 256), BF16), vm((4, 256, 1024), BF16),
        vm((4, 2, 2, 2, 256, 256), BF16), vm((4, 2, 2, 2, 256, 256), BF16), vm((4, 2, 2, 2, 64, 256), BF16),
        vm((features, 256), BF16), vm((4, 2, 64, features), BF16),
        vm((2, 256, 256), F32), vm((2, 256, HEAD), BF16), vm((2, 256, HEAD), BF16),
        vm((2, 256, 256), BF16), vm((2, 256, 256), BF16),
        vm((2, 256, 256), F32), vm((2, 256, HEAD), BF16), vm((2, 256, HEAD), BF16),
        vm((4, 2, 64, features), F32), vm((4, 64, features), BF16), vm((4, 64, features), BF16),
        vm((64, 256), BF16), vm((4, 64, 256), BF16), vm((4, 64, 256), BF16), vm((4, 64, 256), BF16),
        vm((2, 256, 256), BF16), vm((2, 256, 256), F32),
        vm((2, 256, HEAD), F32), vm((2, 256, HEAD), BF16), vm((2, 256, HEAD), F32),
        vm((2, 256, HEAD), BF16), vm((2, 256, 256), BF16),
        vm((8, 2, 256, 256), F32), vm((8, 2, 256, 256), F32), vm((8, 2, 64, 256), F32), vm((64, 256), F32),
    ]
    scratch += scatter_bufs(256) + scatter_bufs(256) + scatter_bufs(64)
    scratch += [dma(4), dma(4)] * 3
    scratch += [dma(4), dma(4), dma(4), dma(12), dma(1), dma(4)] * 3
    scratch += [dma(1), dma(4), dma(12), dma(12), dma(4), dma(4)] * 3
    scratch += [dma(10), dma(10), dma(3), dma(4), dma(3), dma(4), dma(2)]
    whole = pl.BlockSpec(memory_space=pltpu.VMEM)
    hbm = pl.BlockSpec(memory_space=pl.ANY)
    update, grad_text, grad_vision = pl.pallas_call(
        kernel,
        out_shape=(
            jax.ShapeDtypeStruct((256, 256), BF16),
            jax.ShapeDtypeStruct((256, 256), BF16),
            jax.ShapeDtypeStruct((features, 256), BF16),
        ),
        in_specs=[hbm, hbm, whole, whole, hbm, whole, whole, hbm],
        out_specs=(whole,) * 3,
        scratch_shapes=scratch,
        name="cross_attention",
        compiler_params=pltpu.CompilerParams(
            collective_id=0, has_side_effects=True, vmem_limit_bytes=60 * 2**20
        ),
    )(
        text, grad_out, vision.T, gate.reshape(1, 1),
        w_query, w_key, w_value, w_out,
    )
    return update, grad_text, grad_vision.T


def solution(mesh):
    return jax.shard_map(
        body,
        mesh=mesh,
        in_specs=(
            P("dp", "tensor"), P("dp", "tensor"), P("dp", "tensor"), P(),
            P("dp", "tensor"), P("tensor", "dp"), P("tensor", "dp"), P("tensor", "dp"),
        ),
        out_specs=(P("dp", "tensor"), P("dp", "tensor"), P("dp", "tensor")),
        check_vma=False,
    )
```

```python
import jax
import jax.numpy as jnp
from jax import lax
from jax.experimental import pallas as pl
from jax.experimental.pallas import tpu as pltpu
from jax.sharding import PartitionSpec as P

HEAD = 128
EPS = 1e-05
MESH = pl.DeviceIdType.MESH
F32 = jnp.float32
BF16 = jnp.bfloat16
OFFSETS = (0, 3, 1, 2)
NT = (((1,), (1,)), ((), ()))
TN = (((0,), (0,)), ((), ()))


def dot(a, b, dims=(((1,), (0,)), ((), ()))):
    return lax.dot_general(a, b, dims, preferred_element_type=F32)


class Here:
    def __init__(self):
        d, t = lax.axis_index("dp"), lax.axis_index("tensor")
        self.x, self.zl = d // 2, d % 2
        self.y, self.zh, self.c = t // 8, (t // 2) % 4, t % 2
        self.z = 2 * self.zh + self.zl
        self.half = self.zh // 2
        self.kept = self.zl == self.half
        self.place = jnp.where(self.zl == 0, self.z, 7 - self.z) // 2
        self.next_z = (self.z + jnp.where(self.place == 2, 2, -2) * (1 - 2 * self.zl)) % 8
        self.toward = 1 - 2 * self.half

    def order(self, i):
        u = self.place
        table = ((0, 1, 2, 3), (2, 1, 3, 0), (3, 2, 0, 1), (0, 1, 2, 3))
        j = table[3][i]
        for n in (2, 1, 0):
            j = jnp.where(u == n, table[n][i], j)
        return jnp.where(self.zl == 0, j, 3 - j)

    def at(self, dx=0, dy=0, z=None, c=None):
        x = (self.x + dx) % 4 if dx else self.x
        y = (self.y + dy) % 4 if dy else self.y
        z = self.z if z is None else z
        c = self.c if c is None else c
        return (x * 2 + z % 2, y * 8 + (z // 2) * 2 + c)


def rcopy(src, dst, send, recv, device):
    return pltpu.make_async_remote_copy(
        src_ref=src, dst_ref=dst, send_sem=send, recv_sem=recv, device_id=device, device_id_type=MESH
    )


class Sends:
    def __init__(self):
        self.waits = []

    def start(self, *args):
        copy = rcopy(*args)
        copy.start()
        self.waits.append(copy.wait_send)

    def start_if(self, cond, *args):
        @pl.when(cond)
        def _():
            rcopy(*args).start()

        def finish():
            @pl.when(cond)
            def _():
                rcopy(*args).wait_send()

        self.waits.append(finish)

    def finish(self):
        for wait in self.waits:
            wait()


def arrived(dst, sem):
    pltpu.make_async_copy(dst, dst, sem).wait()


class RingGather:
    def __init__(self, me, sends, own, buf, cut, sems):
        self.me, self.sends, self.own, self.buf, self.cut = me, sends, own, buf, cut
        self.ss, self.rs = sems

    def start(self):
        me = self.me
        for way, dx in enumerate((1, -1)):
            self.sends.start(self.own, self.buf.at[me.x], self.ss.at[way], self.rs.at[way], me.at(dx=dx))

    def part(self, slot, way):
        rows = self.buf.shape[1]
        lo, n = ((0, self.cut), (self.cut, rows - self.cut))[way]
        return self.buf.at[slot, pl.ds(lo, n)]

    def relay(self, way):
        me, dx = self.me, (1, -1)[way]
        slot = (me.x - dx) % 4
        arrived(self.buf.at[slot], self.rs.at[way])
        block = self.part(slot, way)
        self.sends.start(block, block, self.ss.at[2 + way], self.rs.at[2 + way], me.at(dx=dx))

    def finish(self):
        for way in range(2):
            arrived(self.part((self.me.x + 2) % 4, way), self.rs.at[2 + way])


class Gather:
    def __init__(self, me, sends, own, buf, sems):
        self.me, self.sends, self.own, self.buf = me, sends, own, buf
        self.zs, self.zr, self.ys, self.yr, self.cs, self.cr = sems

    def start_z(self):
        me = self.me
        dst = self.buf.at[me.y, me.zh % 2, me.c, me.zl]
        recv = self.zr.at[(me.zh % 2) * 2 + me.zl]
        one = me.toward * jnp.where(me.kept, -2, 1)
        args = [
            (self.own, dst, self.zs.at[i], recv, me.at(z=(me.z + sign * one) % 8)) for i, sign in enumerate((1, -1))
        ]
        for arg in args:
            self.sends.start(*arg)

        @pl.when(me.kept)
        def _():
            pltpu.make_async_copy(self.own, dst, recv).start()

    def direct_z(self):
        me = self.me
        dst = self.buf.at[me.y, me.zh % 2, me.c, me.zl]
        recv = self.zr.at[(me.zh % 2) * 2 + me.zl]
        for i in range(4):
            z = me.half + 2 * i
            self.sends.start_if(z != me.z, self.own, dst, self.zs.at[i], recv, me.at(z=z))

        @pl.when(me.kept)
        def _():
            pltpu.make_async_copy(self.own, dst, recv).start()

    def relay_z(self, i):
        if i == 3:
            return
        me = self.me
        cond = (me.place >= 2, me.place != 1, me.place == 1)[i]
        block, sem = self.block(me.y, i), self.zs.at[2 + i % 2]
        args = block, block, sem, self.zr.at[me.order(i)], me.at(z=me.next_z)

        self.sends.start_if(cond, *args)

    def block(self, slot, i):
        j = self.me.order(i)
        return self.buf.at[slot, j // 2, self.me.c, j % 2]

    def to_core(self, slot, r, i):
        block = self.block(slot, i)
        rcopy(block, block, self.cs.at[0], self.cr.at[r], self.me.at(c=1 - self.me.c)).start()

    def arrive(self, *positions, relay=True):
        for i in positions:
            arrived(self.block(self.me.y, i), self.zr.at[self.me.order(i)])
            if relay:
                self.relay_z(i)

    def start_y(self, *positions):
        me = self.me
        for i in positions:
            block = self.block(me.y, i)
            for way, dy in enumerate((1, -1)):
                rcopy(block, block, self.ys.at[way], self.yr.at[way * 4 + i], me.at(dy=dy)).start()
            self.to_core(me.y, 0, i)

    def near(self, *positions):
        me = self.me
        for i in positions:
            for way, dy in enumerate((1, -1)):
                slot = (me.y - dy) % 4
                block = self.block(slot, i)
                arrived(block, self.yr.at[way * 4 + i])
                if way == i % 2:
                    rcopy(block, block, self.ys.at[2 + way], self.yr.at[8 + i], me.at(dy=dy)).start()
                self.to_core(slot, 1 + way, i)

    def far(self, *positions):
        slot = (self.me.y + 2) % 4
        for i in positions:
            arrived(self.block(slot, i), self.yr.at[8 + i])
            self.to_core(slot, 3, i)

    def from_core(self, *rs):
        me = self.me
        for r in rs:
            arrived(self.buf.at[(me.y + OFFSETS[r]) % 4, :, 1 - me.c], self.cr.at[r])
        if 3 in rs:
            self.sends.waits.append(self.sent)

    def sent(self):
        c = self.me.c
        arrived(self.buf.at[:, :, c], self.cs.at[0])
        for way in range(2):
            arrived(self.buf.at[0, :, c], self.ys.at[way])
            arrived(self.buf.at[0, 0, c], self.ys.at[2 + way])


class Scatter:
    def __init__(self, me, sends, compute, acc, bufs, sems):
        self.me, self.sends, self.compute, self.acc = me, sends, compute, acc
        self.pst, self.prv, self.fst, self.frv, self.nst, self.nrv, self.zst, self.zrv, self.tot = bufs
        self.cs, self.cr, self.ys, self.yr, self.zs, self.zr = sems

    def to_core(self, *rs):
        me = self.me
        for r in rs:

            def step(k, _):
                s = r * 2 + k
                self.pst[s] = self.compute((me.y + OFFSETS[r]) % 4, k, 1 - me.c).astype(BF16)
                rcopy(self.pst.at[s], self.prv.at[s], self.cs.at[0], self.cr.at[r], me.at(c=1 - me.c)).start()
                return 0

            lax.fori_loop(0, 2, step, 0)

    def from_core(self, r):
        me = self.me
        arrived(self.prv.at[pl.ds(r * 2, 2)], self.cr.at[r])

        def step(k, _):
            s = r * 2 + k
            value = self.compute((me.y + OFFSETS[r]) % 4, k, me.c) + self.prv[s].astype(F32)
            self.acc[s] = value.reshape(self.acc.shape[1:])
            return 0

        lax.fori_loop(0, 2, step, 0)

    def mine(self, r, i):
        j = self.me.order(3 - i)
        return self.acc[r * 2 + j // 2, j % 2]

    def send_far(self, *positions):
        for i in positions:
            self.fst[i] = self.mine(3, i).astype(BF16)
            self.sends.start(
                self.fst.at[i], self.frv.at[i], self.ys.at[8 + i], self.yr.at[8 + i], self.me.at(dy=(1, -1)[i % 2])
            )

    def near(self, *items):
        me = self.me
        for way, i in items:
            s = way * 4 + i
            value = self.mine(2 - way, i)
            if i % 2 == way:
                arrived(self.frv.at[i], self.yr.at[8 + i])
                value = value + self.frv[i].astype(F32)
            self.nst[s] = value.astype(BF16)
            self.sends.start(self.nst.at[s], self.nrv.at[s], self.ys.at[s], self.yr.at[s], me.at(dy=(1, -1)[way]))

    def z_args(self, i):
        me = self.me
        place = me.place
        j = me.order(3 - i)
        if i < 3:
            passes = (place != 1, place >= 2, place == 3)[i]
            there = (jnp.where(place == 0, 1, place), 5 - place, 2)[i]
            back = (place == 3) if i < 2 else False
            via = (me.z + jnp.where(back, -2, 2) * (1 - 2 * me.zl)) % 8
        else:
            passes, there, via = False, 0, 0
        second = jnp.where(me.zl == 0, 1, 2)
        final = jnp.where(place == 1, jnp.where(j == second, 1, 0), jnp.where(place == 0, 0, 1))
        slot = jnp.where(passes, 2 + there, final)
        z = jnp.where(passes, via, 4 * me.zl + j)
        return self.zst.at[i], self.zrv.at[slot], self.zs.at[i], self.zr.at[slot], me.at(z=z)

    def start_z(self, *positions):
        me = self.me
        place = me.place
        for i in positions:
            total = self.mine(0, i)
            for way in range(2):
                s = way * 4 + i
                arrived(self.nrv.at[s], self.yr.at[s])
                total = total + self.nrv[s].astype(F32)
            adds = (None, place == 1, place != 1, place >= 2)[i]
            if adds is None:
                self.zst[i] = total.astype(BF16)
            else:
                self.tot[i // 3] = total

                @pl.when(adds)
                def _():
                    arrived(self.zrv.at[2 + i], self.zr.at[2 + i])
                    self.tot[i // 3] += self.zrv[2 + i].astype(F32)

                self.zst[i] = self.tot[i // 3].astype(BF16)
            if i < 3:
                rcopy(*self.z_args(i)).start()
            else:
                pl.when(jnp.logical_not(me.kept))(lambda: rcopy(*self.z_args(3)).start())

    def sent_z(self):
        for i in range(3):
            rcopy(*self.z_args(i)).wait_send()
        pl.when(jnp.logical_not(self.me.kept))(lambda: rcopy(*self.z_args(3)).wait_send())

    def direct_z(self, *positions):
        me = self.me
        for i in positions:
            total = self.mine(0, i)
            for way in range(2):
                s = way * 4 + i
                arrived(self.nrv.at[s], self.yr.at[s])
                total = total + self.nrv[s].astype(F32)
            self.zst[i] = total.astype(BF16)
            z = 4 * me.zl + me.order(3 - i)
            there, recv = self.zrv.at[me.zh], self.zr.at[me.zh]
            args = self.zst.at[i], there, self.zs.at[i], recv, me.at(z=z)
            if i < 3:
                self.sends.start(*args)
            else:
                self.sends.start_if(jnp.logical_not(me.kept), *args)

                @pl.when(me.kept)
                def _():
                    pltpu.make_async_copy(self.zst.at[3], there, recv).start()

    def total(self):
        value = jnp.where(self.me.kept, self.tot[1], 0.0)
        for s in range(2):
            arrived(self.zrv.at[s], self.zr.at[s])
            value = value + self.zrv[s].astype(F32)
        return value

    def direct_total(self):
        value = None
        for s in range(4):
            arrived(self.zrv.at[s], self.zr.at[s])
            term = self.zrv[s].astype(F32)
            value = term if value is None else value + term
        return value

    def both_z(self, *positions):
        me = self.me
        for i in positions:
            total = self.mine(0, i)
            for way in range(2):
                s = way * 4 + i
                arrived(self.nrv.at[s], self.yr.at[s])
                total = total + self.nrv[s].astype(F32)
            self.zst[i] = total.astype(BF16)
            j = me.order(3 - i)
            there = (j // 2) * 4 + me.zh
            for k in range(2):
                z = 4 * me.zl + 2 * k + j % 2
                args = self.zst.at[i], self.zrv.at[there], self.zs.at[i * 2 + k], self.zr.at[there], me.at(z=z)
                self.sends.start_if(z != me.z, *args)
                local = pltpu.make_async_copy(*args[:2], args[3])
                pl.when(z == me.z)(local.start)

    def both_total(self, k):
        value = None
        for s in range(4):
            arrived(self.zrv.at[k * 4 + s], self.zr.at[k * 4 + s])
            term = self.zrv[k * 4 + s].astype(F32)
            value = term if value is None else value + term
        return value


def kernel(
    text, grad_out, vision, gate, w_query, w_key, w_value, w_out, update, grad_text, grad_vision,
    wkv_g, wq_g, wo_g, text_g, grad_g, kvg_g, vis_g, vis_r,
    q_acc, q_st, q_rv, att_g, dq_g, ag_acc, ag_st, ag_rv, gv_acc, gv_st, gv_rv, jg, kv_all, kvp, kvp_rv,
    probs_low, probs, query, query_low, query_scale, attend_grad, score_grad, acc_o, acc_t, acc_v, own_kv,
    *rest,
):
    o_bufs, t_bufs, v_bufs = rest[0:9], rest[9:18], rest[18:27]
    rest = rest[27:]
    x_sems = [rest[2 * i : 2 * i + 2] for i in range(3)]
    rest = rest[6:]
    g_sems = [rest[6 * i : 6 * i + 6] for i in range(3)]
    rest = rest[18:]
    r_sems = [rest[6 * i : 6 * i + 6] for i in range(3)]
    rest = rest[18:]
    e_ss, e_rs, m_ss, m_rs, n_ss, n_rs, l_sem = rest

    me = Here()
    sends = Sends()
    zp = me.zl + 2 * me.zh + 1 - 2 * me.zl
    piece = (me.zh % 2) * 2 + me.c
    near_y = [(me.y + off) % 4 for off in OFFSETS]

    def exchange(i, src, dst):
        sends.start(src, dst, e_ss.at[i], e_rs.at[i], me.at(z=zp))

    def mate(j):
        p = (piece + 1 + j) % 4
        return p, me.at(z=me.half * 4 + (p // 2) * 2 + me.zl, c=p % 2)

    gx_kv = RingGather(me, sends, wkv_g.at[me.x], wkv_g, 128, x_sems[0])
    gx_q = RingGather(me, sends, w_query, wq_g, 512, x_sems[1])
    gx_o = RingGather(me, sends, w_out, wo_g, 128, x_sems[2])
    g_text = Gather(me, sends, text, text_g, g_sems[0])
    g_grad = Gather(me, sends, grad_out, grad_g, g_sems[1])
    g_kv = Gather(me, sends, jg, kvg_g, g_sems[2])

    barrier = pltpu.get_barrier_semaphore()
    around = [me.at(dx=1), me.at(dx=-1), me.at(dy=1), me.at(dy=-1), me.at(z=zp)]
    around += [mate(j)[1] for j in range(3)]
    for device in around:
        pl.semaphore_signal(barrier, inc=1, device_id=device, device_id_type=MESH)
    for i in range(4):
        for z in (me.half + 2 * i, 4 * me.zl + i):

            @pl.when(z != me.z)
            def _():
                pl.semaphore_signal(barrier, inc=1, device_id=me.at(z=z), device_id_type=MESH)

    @pl.when(jnp.logical_not(me.kept))
    def _():
        pl.semaphore_signal(barrier, inc=1, device_id=me.at(z=me.next_z), device_id_type=MESH)

    local_q = pltpu.make_async_copy(w_query, wq_g.at[me.x], l_sem.at[0])
    local_o = pltpu.make_async_copy(w_out, wo_g.at[me.x], l_sem.at[1])
    local_q.start()
    local_o.start()
    wkv_g[me.x, :, :HEAD] = w_key[...]
    wkv_g[me.x, :, HEAD:] = w_value[...]
    pl.semaphore_wait(barrier, jnp.where(me.kept, 14, 17))

    g_text.start_z()
    gx_kv.start()
    exchange(0, vision, vis_g)

    def kv_block(slot, k, cc):
        return dot(vis_r[k * 2 + cc].reshape(128, vis_r.shape[3]), wkv_g[slot])

    @pl.when(me.kept)
    def _():
        arrived(g_text.block(me.y, 0), g_text.zr.at[me.order(0)])
        g_text.start_y(0)

    vis_r[:, me.zl] = vision[...].T.reshape(4, 64, -1)
    gx_kv.relay(0)
    gx_kv.relay(1)
    gx_q.start()

    @pl.when(jnp.logical_not(me.kept))
    def _():
        arrived(g_text.block(me.y, 0), g_text.zr.at[me.order(0)])
        g_text.start_y(0)

    g_text.relay_z(0)
    g_text.arrive(1)
    g_text.start_y(1)
    g_text.near(0)
    g_text.arrive(2)
    g_text.start_y(2)
    with jax.named_scope("vis_wait"):
        arrived(vis_g, e_rs.at[0])
    vis_r[:, 1 - me.zl] = vis_g[...].T.reshape(4, 64, -1)
    gx_kv.finish()
    s_kv = Scatter(me, sends, kv_block, acc_v, v_bufs, r_sems[2])
    s_kv.to_core(3, 2, 1, 0)
    sends.waits.append(lambda: arrived(s_kv.pst, s_kv.cs.at[0]))
    g_text.near(1)
    g_text.arrive(3)
    g_text.start_y(3)
    g_grad.start_z()
    s_kv.from_core(3)
    s_kv.send_far(0, 1, 2, 3)
    s_kv.from_core(2)
    s_kv.from_core(1)
    s_kv.near((0, 1), (1, 0), (0, 3), (1, 2))
    s_kv.from_core(0)
    g_text.near(2)
    gx_q.relay(0)
    gx_q.relay(1)
    gx_o.start()
    s_kv.near((0, 0), (1, 1), (0, 2), (1, 3))
    g_text.near(3)
    g_grad.arrive(0)
    g_grad.start_y(0)
    s_kv.both_z(0, 1, 2, 3)
    g_grad.arrive(1)
    g_grad.start_y(1)
    g_text.far(0, 1, 2, 3)
    g_text.from_core(0, 1, 2)
    def q_part(slot):
        total = None
        for j in range(4):
            term = dot(text_g[slot, j // 2, j % 2].reshape(512, 256), wq_g[slot, pl.ds(j * 256, 256), :])
            total = term if total is None else total + term
        return total.reshape(2, 256, 256)

    local_q.wait()
    gx_q.finish()
    with jax.named_scope("query"):
        q_acc[...] = q_part(near_y[0])
        q_acc[...] += q_part(near_y[1])
        q_acc[...] += q_part(near_y[2])
    g_grad.arrive(2)
    g_grad.start_y(2)
    g_text.from_core(3)
    with jax.named_scope("query_last"):
        q_acc[...] += q_part(near_y[3])
        for h in range(2):
            q_st[h] = q_acc[1 - me.zl, :, h * HEAD : (h + 1) * HEAD].astype(BF16)
            exchange(1 + h, q_st.at[h], q_rv.at[h])
    g_grad.arrive(3)
    g_grad.start_y(3)
    g_grad.near(0)
    gx_o.relay(0)
    gx_o.relay(1)
    with jax.named_scope("kv"):
        rows = []
        for k in range(2):
            projected = s_kv.both_total(k)
            rows.append(projected)
            keys = projected[:, :HEAD]
            key_scale = lax.rsqrt(jnp.mean(keys * keys, axis=-1, keepdims=True) + EPS)
            p = k * 2 + me.c
            kv_all[p, :, :HEAD] = (keys * key_scale).astype(BF16)
            kv_all[p, :, HEAD:] = projected[:, HEAD:].astype(BF16)
            sends.start(kv_all.at[p], kv_all.at[p], m_ss.at[k], m_rs.at[k], me.at(c=1 - me.c))
        own_kv[...] = jnp.where(me.zh % 2 == 0, rows[0], rows[1])

    g_grad.near(1)
    with jax.named_scope("kv_wait"):
        for k in range(2):
            arrived(kv_all.at[k * 2 + 1 - me.c], m_rs.at[k])
    kv = kv_all[...].reshape(256, 256)
    key_head, value_head = kv[:, :HEAD], kv[:, HEAD:]
    scale = HEAD ** (-0.5)
    tanh_gate = jnp.tanh(gate[...])

    for h in range(2):
        own = slice(h * HEAD, (h + 1) * HEAD)
        with jax.named_scope("q_wait"):
            arrived(q_rv.at[h], e_rs.at[1 + h])
        with jax.named_scope("attention"):
            q = q_acc[me.zl, :, own] + q_rv[h].astype(F32)
            q_scale = lax.rsqrt(jnp.mean(q * q, axis=-1, keepdims=True) + EPS)
            q_normed = (q * q_scale).astype(BF16)
            query[h] = q
            query_low[h] = q_normed
            query_scale[h] = jnp.broadcast_to(q_scale, q.shape)
            expo = jnp.exp(dot(q_normed, key_head, NT) * scale)
            prob = expo / jnp.sum(expo, axis=-1, keepdims=True)
            probs[h] = prob
            low = prob.astype(BF16)
            probs_low[h] = low
            att_g[me.zl, :, own] = dot(low, value_head).astype(BF16)
            exchange(3 + h, att_g.at[me.zl, :, own], att_g.at[me.zl, :, own])
        g_grad.near(2 + h)

    def ag_part(slot):
        total = None
        for j in range(4):
            term = dot(grad_g[slot, j // 2, j % 2].reshape(512, 256), wo_g[slot, :, pl.ds(j * 256, 256)], NT)
            total = term if total is None else total + term
        return total.reshape(2, 256, 256)

    local_o.wait()
    gx_o.finish()

    def out_block(slot, k, cc):
        block = wo_g[slot, :, pl.ds(pl.multiple_of((k * 2 + cc) * 256, 256), 256)]
        return dot(att_g[...].reshape(512, 256), block)

    with jax.named_scope("att_wait"):
        for h in range(2):
            theirs = att_g.at[1 - me.zl, :, pl.ds(h * HEAD, HEAD)]
            arrived(theirs, e_rs.at[3 + h])
    s_out = Scatter(me, sends, out_block, acc_o, o_bufs, r_sems[0])
    s_out.to_core(3)
    s_out.to_core(2)
    s_out.from_core(3)
    s_out.send_far(0, 1)
    s_out.to_core(1)
    s_out.from_core(2)
    s_out.near((0, 1))
    s_out.from_core(1)
    s_out.near((1, 0))
    s_out.send_far(2, 3)
    g_grad.from_core(0, 1, 2)
    with jax.named_scope("attend_grad"):
        ag_acc[...] = ag_part(near_y[0])
        ag_acc[...] += ag_part(near_y[1])
        ag_acc[...] += ag_part(near_y[2])
    g_grad.far(0, 1, 2, 3)
    g_grad.from_core(3)
    with jax.named_scope("attend_grad_last"):
        ag_acc[...] += ag_part(near_y[3])
        for h in range(2):
            ag_st[h] = ag_acc[1 - me.zl, :, h * HEAD : (h + 1) * HEAD].astype(BF16)
            exchange(5 + h, ag_st.at[h], ag_rv.at[h])
    s_out.near((0, 0), (1, 1), (0, 3), (1, 2))
    s_out.to_core(0)
    sends.waits.append(lambda: arrived(s_out.pst, s_out.cs.at[0]))
    s_out.from_core(0)

    for h in range(2):
        own = slice(h * HEAD, (h + 1) * HEAD)
        with jax.named_scope("ag_wait"):
            arrived(ag_rv.at[h], e_rs.at[5 + h])
        with jax.named_scope("backward"):
            a_grad = (tanh_gate * (ag_acc[me.zl, :, own] + ag_rv[h].astype(F32))).astype(BF16)
            attend_grad[h] = a_grad
            prob = probs[h]
            prob_grad = dot(a_grad, value_head, NT)
            delta = jnp.sum(prob * prob_grad, axis=-1, keepdims=True)
            s_grad = (prob * (prob_grad - delta) * scale).astype(BF16)
            score_grad[h] = s_grad
            normed_grad = dot(s_grad, key_head)
            q, q_scale = query[h], query_scale[h]
            mean = jnp.mean(normed_grad * q, axis=-1, keepdims=True)
            q_grad = q_scale * (normed_grad - q * (q_scale * q_scale) * mean)
            dq_g[me.zl, :, own] = q_grad.astype(BF16)
        exchange(7 + h, dq_g.at[me.zl, :, own], dq_g.at[me.zl, :, own])
        if h == 0:
            s_out.near((0, 2), (1, 3))
    with jax.named_scope("kv_part"):
        key_part = dot(score_grad[0], query_low[0], TN) + dot(score_grad[1], query_low[1], TN)
        value_part = dot(probs_low[0], attend_grad[0], TN) + dot(probs_low[1], attend_grad[1], TN)
        kvp[:, :, :HEAD] = key_part.astype(BF16).reshape(4, 64, HEAD)
        kvp[:, :, HEAD:] = value_part.astype(BF16).reshape(4, 64, HEAD)
        for j in range(3):
            p, device = mate(j)
            sends.start(kvp.at[p], kvp_rv.at[piece], n_ss.at[j], n_rs.at[piece], device)

    def text_block(slot, k, cc):
        block = wq_g[slot, pl.ds(pl.multiple_of((k * 2 + cc) * 256, 256), 256), :]
        return dot(dq_g[...].reshape(512, 256), block, NT)

    with jax.named_scope("dq_wait"):
        for h in range(2):
            theirs = dq_g.at[1 - me.zl, :, pl.ds(h * HEAD, HEAD)]
            arrived(theirs, e_rs.at[7 + h])
    s_text = Scatter(me, sends, text_block, acc_t, t_bufs, r_sems[1])
    s_text.to_core(3)
    s_text.to_core(2)
    s_text.from_core(3)
    s_text.send_far(0, 1)

    with jax.named_scope("kv_grad"):
        kv_grad = kvp[piece].astype(F32)
        for j in range(3):
            p, _ = mate(j)
            arrived(kvp_rv.at[p], n_rs.at[p])
            kv_grad = kv_grad + kvp_rv[p].astype(F32)
        keys = own_kv[:, :HEAD]
        key_scale = lax.rsqrt(jnp.mean(keys * keys, axis=-1, keepdims=True) + EPS)
        k_grad = kv_grad[:, :HEAD]
        mean = jnp.mean(k_grad * keys, axis=-1, keepdims=True)
        k_grad = key_scale * k_grad - keys * (key_scale * key_scale * key_scale) * mean
        jg[:, :HEAD] = k_grad.astype(BF16)
        jg[:, HEAD:] = kv_grad[:, HEAD:].astype(BF16)
        g_kv.direct_z()

    s_text.to_core(1)
    s_out.direct_z(0, 1)
    s_text.from_core(2)
    s_text.near((0, 1))
    s_text.from_core(1)
    s_text.near((1, 0))

    s_text.near((0, 0), (1, 1))
    s_text.send_far(2, 3)
    s_out.direct_z(2, 3)
    s_text.to_core(0)
    sends.waits.append(lambda: arrived(s_text.pst, s_text.cs.at[0]))
    s_text.from_core(0)
    g_kv.arrive(0, 1, 2, 3, relay=False)
    g_kv.start_y(0, 1, 2, 3)
    s_text.near((0, 3), (1, 2))
    s_text.direct_z(0, 1)
    s_text.near((0, 2), (1, 3))
    g_kv.near(0, 1, 2, 3)
    s_text.direct_z(2, 3)
    g_kv.far(0, 1, 2, 3)
    g_kv.from_core(0, 1, 2, 3)

    with jax.named_scope("vision_grad"):
        gv = None
        for i in range(4):
            term = dot(kvg_g[i].reshape(512, 256), wkv_g[i], NT)
            gv = term if gv is None else gv + term
        gv_acc[...] = gv.reshape(4, 2, 64, -1)
        gv_st[...] = gv_acc[:, 1 - me.zl].astype(BF16)
        exchange(9, gv_st, gv_rv)
    with jax.named_scope("update"):
        update[...] = (tanh_gate * s_out.direct_total()).astype(BF16)
    with jax.named_scope("vision_grad_last"):
        arrived(gv_rv, e_rs.at[9])
        total = gv_acc[:, me.zl] + gv_rv[...].astype(F32)
        grad_vision[...] = total.reshape(256, -1).T.astype(BF16)
    with jax.named_scope("text_grad_last"):
        grad_text[...] = s_text.direct_total().astype(BF16)
    with jax.named_scope("sends"):
        sends.finish()


def hand_on(*refs):
    for n in range(3):
        refs[3 + n][...] = refs[n][...]


def body(text, grad_out, vision, gate, w_query, w_key, w_value, w_out):
    features = vision.shape[1]
    dma = lambda n: pltpu.SemaphoreType.DMA((n,))
    vm = pltpu.VMEM

    def scatter_bufs(m):
        return [
            vm((8, 2 * m, 256), BF16), vm((8, 2 * m, 256), BF16),
            vm((4, m, 256), BF16), vm((4, m, 256), BF16),
            vm((8, m, 256), BF16), vm((8, m, 256), BF16),
            vm((4, m, 256), BF16), vm((8 if m == 64 else 6, m, 256), BF16), vm((2, m, 256), F32),
        ]

    scratch = [
        vm((4, features, 256), BF16), vm((4, 1024, 256), BF16), vm((4, 256, 1024), BF16),
        vm((4, 2, 2, 2, 256, 256), BF16), vm((4, 2, 2, 2, 256, 256), BF16), vm((4, 2, 2, 2, 64, 256), BF16),
        vm((features, 256), BF16), vm((4, 2, 64, features), BF16),
        vm((2, 256, 256), F32), vm((2, 256, HEAD), BF16), vm((2, 256, HEAD), BF16),
        vm((2, 256, 256), BF16), vm((2, 256, 256), BF16),
        vm((2, 256, 256), F32), vm((2, 256, HEAD), BF16), vm((2, 256, HEAD), BF16),
        vm((4, 2, 64, features), F32), vm((4, 64, features), BF16), vm((4, 64, features), BF16),
        vm((64, 256), BF16), vm((4, 64, 256), BF16), vm((4, 64, 256), BF16), vm((4, 64, 256), BF16),
        vm((2, 256, 256), BF16), vm((2, 256, 256), F32),
        vm((2, 256, HEAD), F32), vm((2, 256, HEAD), BF16), vm((2, 256, HEAD), F32),
        vm((2, 256, HEAD), BF16), vm((2, 256, 256), BF16),
        vm((8, 2, 256, 256), F32), vm((8, 2, 256, 256), F32), vm((8, 2, 64, 256), F32), vm((64, 256), F32),
    ]
    scratch += scatter_bufs(256) + scatter_bufs(256) + scatter_bufs(64)
    scratch += [dma(4), dma(4)] * 3
    scratch += [dma(4), dma(4), dma(4), dma(12), dma(1), dma(4)] * 3
    scratch += [dma(1), dma(4), dma(12), dma(12), dma(8), dma(8)] * 3
    scratch += [dma(10), dma(10), dma(2), dma(2), dma(3), dma(4), dma(2)]
    whole = pl.BlockSpec(memory_space=pltpu.VMEM)
    hbm = pl.BlockSpec(memory_space=pl.ANY)
    update, grad_text, grad_vision = pl.pallas_call(
        kernel,
        out_shape=(
            jax.ShapeDtypeStruct((256, 256), BF16),
            jax.ShapeDtypeStruct((256, 256), BF16),
            jax.ShapeDtypeStruct((features, 256), BF16),
        ),
        in_specs=[hbm, hbm, whole, whole, hbm, whole, whole, hbm],
        out_specs=(whole,) * 3,
        scratch_shapes=scratch,
        name="cross_attention",
        compiler_params=pltpu.CompilerParams(
            collective_id=0, has_side_effects=True, vmem_limit_bytes=60 * 2**20
        ),
    )(
        text, grad_out, vision.T, gate.reshape(1, 1),
        w_query, w_key, w_value, w_out,
    )
    update, grad_text, grad_vision = pl.pallas_call(
        hand_on,
        out_shape=(update, grad_text, grad_vision),
        in_specs=[whole] * 3,
        out_specs=(whole,) * 3,
        name="hand_on",
    )(update, grad_text, grad_vision)
    return update, grad_text, grad_vision.T


def solution(mesh):
    return jax.shard_map(
        body,
        mesh=mesh,
        in_specs=(
            P("dp", "tensor"), P("dp", "tensor"), P("dp", "tensor"), P(),
            P("dp", "tensor"), P("tensor", "dp"), P("tensor", "dp"), P("tensor", "dp"),
        ),
        out_specs=(P("dp", "tensor"), P("dp", "tensor"), P("dp", "tensor")),
        check_vma=False,
    )
```

```python
import jax
import jax.numpy as jnp
from jax import lax
from jax.experimental import pallas as pl
from jax.experimental.pallas import tpu as pltpu
from jax.sharding import PartitionSpec as P

HEAD = 128
EPS = 1e-05
MESH = pl.DeviceIdType.MESH
F32 = jnp.float32
BF16 = jnp.bfloat16
OFFSETS = (0, 3, 1, 2)
NT = (((1,), (1,)), ((), ()))
TN = (((0,), (0,)), ((), ()))


def dot(a, b, dims=(((1,), (0,)), ((), ()))):
    return lax.dot_general(a, b, dims, preferred_element_type=F32)


class Here:
    def __init__(self):
        d, t = lax.axis_index("dp"), lax.axis_index("tensor")
        self.x, self.zl = d // 2, d % 2
        self.y, self.zh, self.c = t // 8, (t // 2) % 4, t % 2
        self.z = 2 * self.zh + self.zl
        self.half = self.zh // 2
        self.kept = self.zl == self.half
        self.place = jnp.where(self.zl == 0, self.z, 7 - self.z) // 2
        self.next_z = (self.z + jnp.where(self.place == 2, 2, -2) * (1 - 2 * self.zl)) % 8
        self.toward = 1 - 2 * self.half

    def order(self, i):
        u = self.place
        table = ((0, 1, 2, 3), (2, 1, 3, 0), (3, 2, 0, 1), (0, 1, 2, 3))
        j = table[3][i]
        for n in (2, 1, 0):
            j = jnp.where(u == n, table[n][i], j)
        return jnp.where(self.zl == 0, j, 3 - j)

    def at(self, dx=0, dy=0, z=None, c=None):
        x = (self.x + dx) % 4 if dx else self.x
        y = (self.y + dy) % 4 if dy else self.y
        z = self.z if z is None else z
        c = self.c if c is None else c
        return (x * 2 + z % 2, y * 8 + (z // 2) * 2 + c)


def rcopy(src, dst, send, recv, device):
    return pltpu.make_async_remote_copy(
        src_ref=src, dst_ref=dst, send_sem=send, recv_sem=recv, device_id=device, device_id_type=MESH
    )


class Sends:
    def __init__(self):
        self.waits = []

    def start(self, *args):
        copy = rcopy(*args)
        copy.start()
        self.waits.append(copy.wait_send)

    def start_if(self, cond, *args):
        @pl.when(cond)
        def _():
            rcopy(*args).start()

        def finish():
            @pl.when(cond)
            def _():
                rcopy(*args).wait_send()

        self.waits.append(finish)

    def finish(self):
        for wait in self.waits:
            wait()


def arrived(dst, sem):
    pltpu.make_async_copy(dst, dst, sem).wait()


class RingGather:
    def __init__(self, me, sends, own, buf, cut, sems):
        self.me, self.sends, self.own, self.buf, self.cut = me, sends, own, buf, cut
        self.ss, self.rs = sems

    def start(self):
        me = self.me
        for way, dx in enumerate((1, -1)):
            self.sends.start(self.own, self.buf.at[me.x], self.ss.at[way], self.rs.at[way], me.at(dx=dx))

    def part(self, slot, way):
        rows = self.buf.shape[1]
        lo, n = ((0, self.cut), (self.cut, rows - self.cut))[way]
        return self.buf.at[slot, pl.ds(lo, n)]

    def relay(self, way):
        me, dx = self.me, (1, -1)[way]
        slot = (me.x - dx) % 4
        arrived(self.buf.at[slot], self.rs.at[way])
        block = self.part(slot, way)
        self.sends.start(block, block, self.ss.at[2 + way], self.rs.at[2 + way], me.at(dx=dx))

    def finish(self):
        for way in range(2):
            arrived(self.part((self.me.x + 2) % 4, way), self.rs.at[2 + way])


class Gather:
    def __init__(self, me, sends, own, buf, sems):
        self.me, self.sends, self.own, self.buf = me, sends, own, buf
        self.zs, self.zr, self.ys, self.yr, self.cs, self.cr = sems

    def start_z(self):
        me = self.me
        dst = self.buf.at[me.y, me.zh % 2, me.c, me.zl]
        recv = self.zr.at[(me.zh % 2) * 2 + me.zl]
        one = me.toward * jnp.where(me.kept, -2, 1)
        args = [
            (self.own, dst, self.zs.at[i], recv, me.at(z=(me.z + sign * one) % 8)) for i, sign in enumerate((1, -1))
        ]
        for arg in args:
            self.sends.start(*arg)

        @pl.when(me.kept)
        def _():
            pltpu.make_async_copy(self.own, dst, recv).start()

    def direct_z(self):
        me = self.me
        dst = self.buf.at[me.y, me.zh % 2, me.c, me.zl]
        recv = self.zr.at[(me.zh % 2) * 2 + me.zl]
        for i in range(4):
            z = me.half + 2 * i
            self.sends.start_if(z != me.z, self.own, dst, self.zs.at[i], recv, me.at(z=z))

        @pl.when(me.kept)
        def _():
            pltpu.make_async_copy(self.own, dst, recv).start()

    def relay_z(self, i):
        if i == 3:
            return
        me = self.me
        cond = (me.place >= 2, me.place != 1, me.place == 1)[i]
        block, sem = self.block(me.y, i), self.zs.at[2 + i % 2]
        args = block, block, sem, self.zr.at[me.order(i)], me.at(z=me.next_z)

        self.sends.start_if(cond, *args)

    def block(self, slot, i):
        j = self.me.order(i)
        return self.buf.at[slot, j // 2, self.me.c, j % 2]

    def to_core(self, slot, r, i):
        block = self.block(slot, i)
        rcopy(block, block, self.cs.at[0], self.cr.at[r], self.me.at(c=1 - self.me.c)).start()

    def arrive(self, *positions, relay=True):
        for i in positions:
            arrived(self.block(self.me.y, i), self.zr.at[self.me.order(i)])
            if relay:
                self.relay_z(i)

    def start_y(self, *positions):
        me = self.me
        for i in positions:
            block = self.block(me.y, i)
            for way, dy in enumerate((1, -1)):
                rcopy(block, block, self.ys.at[way], self.yr.at[way * 4 + i], me.at(dy=dy)).start()
            self.to_core(me.y, 0, i)

    def near(self, *positions):
        me = self.me
        for i in positions:
            for way, dy in enumerate((1, -1)):
                slot = (me.y - dy) % 4
                block = self.block(slot, i)
                arrived(block, self.yr.at[way * 4 + i])
                if way == i % 2:
                    rcopy(block, block, self.ys.at[2 + way], self.yr.at[8 + i], me.at(dy=dy)).start()
                self.to_core(slot, 1 + way, i)

    def far(self, *positions):
        slot = (self.me.y + 2) % 4
        for i in positions:
            arrived(self.block(slot, i), self.yr.at[8 + i])
            self.to_core(slot, 3, i)

    def from_core(self, *rs):
        me = self.me
        for r in rs:
            arrived(self.buf.at[(me.y + OFFSETS[r]) % 4, :, 1 - me.c], self.cr.at[r])
        if 3 in rs:
            self.sends.waits.append(self.sent)

    def sent(self):
        c = self.me.c
        arrived(self.buf.at[:, :, c], self.cs.at[0])
        for way in range(2):
            arrived(self.buf.at[0, :, c], self.ys.at[way])
            arrived(self.buf.at[0, 0, c], self.ys.at[2 + way])


class Scatter:
    def __init__(self, me, sends, compute, acc, bufs, sems):
        self.me, self.sends, self.compute, self.acc = me, sends, compute, acc
        self.pst, self.prv, self.fst, self.frv, self.nst, self.nrv, self.zst, self.zrv = bufs
        self.cs, self.cr, self.ys, self.yr, self.zs, self.zr = sems

    def to_core(self, *rs):
        me = self.me
        for r in rs:

            def step(k, _):
                s = r * 2 + k
                self.pst[s] = self.compute((me.y + OFFSETS[r]) % 4, k, 1 - me.c).astype(BF16)
                rcopy(self.pst.at[s], self.prv.at[s], self.cs.at[0], self.cr.at[r], me.at(c=1 - me.c)).start()
                return 0

            lax.fori_loop(0, 2, step, 0)

    def from_core(self, r):
        me = self.me
        arrived(self.prv.at[pl.ds(r * 2, 2)], self.cr.at[r])

        def step(k, _):
            s = r * 2 + k
            value = self.compute((me.y + OFFSETS[r]) % 4, k, me.c) + self.prv[s].astype(F32)
            self.acc[s] = value.reshape(self.acc.shape[1:])
            return 0

        lax.fori_loop(0, 2, step, 0)

    def mine(self, r, i):
        j = self.me.order(3 - i)
        return self.acc[r * 2 + j // 2, j % 2]

    def send_far(self, *positions):
        for i in positions:
            self.fst[i] = self.mine(3, i).astype(BF16)
            self.sends.start(
                self.fst.at[i], self.frv.at[i], self.ys.at[8 + i], self.yr.at[8 + i], self.me.at(dy=(1, -1)[i % 2])
            )

    def near(self, *items):
        me = self.me
        for way, i in items:
            s = way * 4 + i
            value = self.mine(2 - way, i)
            if i % 2 == way:
                arrived(self.frv.at[i], self.yr.at[8 + i])
                value = value + self.frv[i].astype(F32)
            self.nst[s] = value.astype(BF16)
            self.sends.start(self.nst.at[s], self.nrv.at[s], self.ys.at[s], self.yr.at[s], me.at(dy=(1, -1)[way]))

    def z_args(self, i):
        me = self.me
        slot = jnp.minimum(me.place, 2)
        z = 4 * me.zl + me.order(3 - i)
        if i < 2:
            passes = me.place >= 2
            slot = jnp.where(passes, 1 + (me.place, 5 - me.place)[i], slot)
            z = jnp.where(passes, me.next_z, z)
        return self.zst.at[i], self.zrv.at[slot], self.zs.at[i], self.zr.at[slot], me.at(z=z)

    def start_z(self, *positions):
        me = self.me
        for i in positions:
            total = self.mine(0, i)
            for way in range(2):
                s = way * 4 + i
                arrived(self.nrv.at[s], self.yr.at[s])
                total = total + self.nrv[s].astype(F32)
            self.zst[i] = total.astype(BF16)
            if i >= 2:

                @pl.when(me.place >= 2)
                def _():
                    arrived(self.zrv.at[1 + i], self.zr.at[1 + i])
                    self.zst[i] = (total + self.zrv[1 + i].astype(F32)).astype(BF16)

            args = self.z_args(i)
            if i < 3:
                self.sends.start(*args)
            else:
                self.sends.start_if(jnp.logical_not(me.kept), *args)

                @pl.when(me.kept)
                def _():
                    pltpu.make_async_copy(args[0], args[1], args[3]).start()

    def total(self):
        value = None
        for s in range(3):
            arrived(self.zrv.at[s], self.zr.at[s])
            term = self.zrv[s].astype(F32)
            value = term if value is None else value + term
        return value

    def both_z(self, *positions):
        me = self.me
        for i in positions:
            total = self.mine(0, i)
            for way in range(2):
                s = way * 4 + i
                arrived(self.nrv.at[s], self.yr.at[s])
                total = total + self.nrv[s].astype(F32)
            self.zst[i] = total.astype(BF16)
            j = me.order(3 - i)
            there = (j // 2) * 4 + me.zh
            for k in range(2):
                z = 4 * me.zl + 2 * k + j % 2
                args = self.zst.at[i], self.zrv.at[there], self.zs.at[i * 2 + k], self.zr.at[there], me.at(z=z)
                self.sends.start_if(z != me.z, *args)
                local = pltpu.make_async_copy(*args[:2], args[3])
                pl.when(z == me.z)(local.start)

    def both_total(self, k):
        value = None
        for s in range(4):
            arrived(self.zrv.at[k * 4 + s], self.zr.at[k * 4 + s])
            term = self.zrv[k * 4 + s].astype(F32)
            value = term if value is None else value + term
        return value


def kernel(
    text, grad_out, vision, gate, w_query, w_key, w_value, w_out, update, grad_text, grad_vision,
    wkv_g, wq_g, wo_g, text_g, grad_g, kvg_g, vis_g, vis_r,
    q_acc, q_st, q_rv, att_g, dq_g, ag_acc, ag_st, ag_rv, gv_acc, gv_st, gv_rv, jg, kv_all, kvp, kvp_rv,
    probs_low, probs, query, query_low, query_scale, attend_grad, score_grad, acc_o, acc_t, acc_v, own_kv,
    *rest,
):
    o_bufs, t_bufs, v_bufs = rest[0:8], rest[8:16], rest[16:24]
    rest = rest[24:]
    x_sems = [rest[2 * i : 2 * i + 2] for i in range(3)]
    rest = rest[6:]
    g_sems = [rest[6 * i : 6 * i + 6] for i in range(3)]
    rest = rest[18:]
    r_sems = [rest[6 * i : 6 * i + 6] for i in range(3)]
    rest = rest[18:]
    e_ss, e_rs, m_ss, m_rs, n_ss, n_rs, l_sem = rest

    me = Here()
    sends = Sends()
    zp = me.zl + 2 * me.zh + 1 - 2 * me.zl
    piece = (me.zh % 2) * 2 + me.c
    near_y = [(me.y + off) % 4 for off in OFFSETS]

    def exchange(i, src, dst):
        sends.start(src, dst, e_ss.at[i], e_rs.at[i], me.at(z=zp))

    def mate(j):
        p = (piece + 1 + j) % 4
        return p, me.at(z=me.half * 4 + (p // 2) * 2 + me.zl, c=p % 2)

    gx_kv = RingGather(me, sends, wkv_g.at[me.x], wkv_g, 128, x_sems[0])
    gx_q = RingGather(me, sends, w_query, wq_g, 512, x_sems[1])
    gx_o = RingGather(me, sends, w_out, wo_g, 128, x_sems[2])
    g_text = Gather(me, sends, text, text_g, g_sems[0])
    g_grad = Gather(me, sends, grad_out, grad_g, g_sems[1])
    g_kv = Gather(me, sends, jg, kvg_g, g_sems[2])

    barrier = pltpu.get_barrier_semaphore()
    around = [me.at(dx=1), me.at(dx=-1), me.at(dy=1), me.at(dy=-1), me.at(z=zp)]
    around += [mate(j)[1] for j in range(3)]
    for device in around:
        pl.semaphore_signal(barrier, inc=1, device_id=device, device_id_type=MESH)
    for i in range(4):
        for z in (me.half + 2 * i, 4 * me.zl + i):

            @pl.when(z != me.z)
            def _():
                pl.semaphore_signal(barrier, inc=1, device_id=me.at(z=z), device_id_type=MESH)

    @pl.when(jnp.logical_not(me.kept))
    def _():
        pl.semaphore_signal(barrier, inc=1, device_id=me.at(z=me.next_z), device_id_type=MESH)

    local_q = pltpu.make_async_copy(w_query, wq_g.at[me.x], l_sem.at[0])
    local_o = pltpu.make_async_copy(w_out, wo_g.at[me.x], l_sem.at[1])
    local_q.start()
    local_o.start()
    wkv_g[me.x, :, :HEAD] = w_key[...]
    wkv_g[me.x, :, HEAD:] = w_value[...]
    pl.semaphore_wait(barrier, jnp.where(me.kept, 14, 17))

    g_text.start_z()
    gx_kv.start()
    exchange(0, vision, vis_g)

    def kv_block(slot, k, cc):
        return dot(vis_r[k * 2 + cc].reshape(128, vis_r.shape[3]), wkv_g[slot])

    @pl.when(me.kept)
    def _():
        arrived(g_text.block(me.y, 0), g_text.zr.at[me.order(0)])
        g_text.start_y(0)

    vis_r[:, me.zl] = vision[...].T.reshape(4, 64, -1)
    gx_kv.relay(0)
    gx_kv.relay(1)
    gx_q.start()

    @pl.when(jnp.logical_not(me.kept))
    def _():
        arrived(g_text.block(me.y, 0), g_text.zr.at[me.order(0)])
        g_text.start_y(0)

    g_text.relay_z(0)
    g_text.arrive(1)
    g_text.start_y(1)
    g_text.near(0)
    g_text.arrive(2)
    g_text.start_y(2)
    with jax.named_scope("vis_wait"):
        arrived(vis_g, e_rs.at[0])
    vis_r[:, 1 - me.zl] = vis_g[...].T.reshape(4, 64, -1)
    gx_kv.finish()
    s_kv = Scatter(me, sends, kv_block, acc_v, v_bufs, r_sems[2])
    s_kv.to_core(3, 2, 1, 0)
    sends.waits.append(lambda: arrived(s_kv.pst, s_kv.cs.at[0]))
    g_text.near(1)
    g_text.arrive(3)
    g_text.start_y(3)
    g_grad.start_z()
    s_kv.from_core(3)
    s_kv.send_far(0, 1, 2, 3)
    s_kv.from_core(2)
    s_kv.from_core(1)
    s_kv.near((0, 1), (1, 0), (0, 3), (1, 2))
    s_kv.from_core(0)
    g_text.near(2)
    gx_q.relay(0)
    gx_q.relay(1)
    gx_o.start()
    s_kv.near((0, 0), (1, 1), (0, 2), (1, 3))
    g_text.near(3)
    g_grad.arrive(0)
    g_grad.start_y(0)
    s_kv.both_z(0, 1, 2, 3)
    g_grad.arrive(1)
    g_grad.start_y(1)
    g_text.far(0, 1, 2, 3)
    g_text.from_core(0, 1, 2)
    def q_part(slot):
        total = None
        for j in range(4):
            term = dot(text_g[slot, j // 2, j % 2].reshape(512, 256), wq_g[slot, pl.ds(j * 256, 256), :])
            total = term if total is None else total + term
        return total.reshape(2, 256, 256)

    local_q.wait()
    gx_q.finish()
    with jax.named_scope("query"):
        q_acc[...] = q_part(near_y[0])
        q_acc[...] += q_part(near_y[1])
        q_acc[...] += q_part(near_y[2])
    g_grad.arrive(2)
    g_grad.start_y(2)
    g_text.from_core(3)
    with jax.named_scope("query_last"):
        q_acc[...] += q_part(near_y[3])
        for h in range(2):
            q_st[h] = q_acc[1 - me.zl, :, h * HEAD : (h + 1) * HEAD].astype(BF16)
            exchange(1 + h, q_st.at[h], q_rv.at[h])
    g_grad.arrive(3)
    g_grad.start_y(3)
    g_grad.near(0)
    gx_o.relay(0)
    gx_o.relay(1)
    with jax.named_scope("kv"):
        rows = []
        for k in range(2):
            projected = s_kv.both_total(k)
            rows.append(projected)
            keys = projected[:, :HEAD]
            key_scale = lax.rsqrt(jnp.mean(keys * keys, axis=-1, keepdims=True) + EPS)
            p = k * 2 + me.c
            kv_all[p, :, :HEAD] = (keys * key_scale).astype(BF16)
            kv_all[p, :, HEAD:] = projected[:, HEAD:].astype(BF16)
            sends.start(kv_all.at[p], kv_all.at[p], m_ss.at[k], m_rs.at[k], me.at(c=1 - me.c))
        own_kv[...] = jnp.where(me.zh % 2 == 0, rows[0], rows[1])

    g_grad.near(1)
    with jax.named_scope("kv_wait"):
        for k in range(2):
            arrived(kv_all.at[k * 2 + 1 - me.c], m_rs.at[k])
    kv = kv_all[...].reshape(256, 256)
    key_head, value_head = kv[:, :HEAD], kv[:, HEAD:]
    scale = HEAD ** (-0.5)
    tanh_gate = jnp.tanh(gate[...])

    for h in range(2):
        own = slice(h * HEAD, (h + 1) * HEAD)
        with jax.named_scope("q_wait"):
            arrived(q_rv.at[h], e_rs.at[1 + h])
        with jax.named_scope("attention"):
            q = q_acc[me.zl, :, own] + q_rv[h].astype(F32)
            q_scale = lax.rsqrt(jnp.mean(q * q, axis=-1, keepdims=True) + EPS)
            q_normed = (q * q_scale).astype(BF16)
            query[h] = q
            query_low[h] = q_normed
            query_scale[h] = jnp.broadcast_to(q_scale, q.shape)
            expo = jnp.exp(dot(q_normed, key_head, NT) * scale)
            prob = expo / jnp.sum(expo, axis=-1, keepdims=True)
            probs[h] = prob
            low = prob.astype(BF16)
            probs_low[h] = low
            att_g[me.zl, :, own] = dot(low, value_head).astype(BF16)
            exchange(3 + h, att_g.at[me.zl, :, own], att_g.at[me.zl, :, own])
        g_grad.near(2 + h)

    def ag_part(slot):
        total = None
        for j in range(4):
            term = dot(grad_g[slot, j // 2, j % 2].reshape(512, 256), wo_g[slot, :, pl.ds(j * 256, 256)], NT)
            total = term if total is None else total + term
        return total.reshape(2, 256, 256)

    local_o.wait()
    gx_o.finish()

    def out_block(slot, k, cc):
        block = wo_g[slot, :, pl.ds(pl.multiple_of((k * 2 + cc) * 256, 256), 256)]
        return dot(att_g[...].reshape(512, 256), block)

    with jax.named_scope("att_wait"):
        for h in range(2):
            theirs = att_g.at[1 - me.zl, :, pl.ds(h * HEAD, HEAD)]
            arrived(theirs, e_rs.at[3 + h])
    s_out = Scatter(me, sends, out_block, acc_o, o_bufs, r_sems[0])
    s_out.to_core(3)
    s_out.to_core(2)
    s_out.from_core(3)
    s_out.send_far(0, 1)
    s_out.to_core(1)
    s_out.from_core(2)
    s_out.near((0, 1))
    s_out.from_core(1)
    s_out.near((1, 0))
    s_out.send_far(2, 3)
    g_grad.from_core(0, 1, 2)
    with jax.named_scope("attend_grad"):
        ag_acc[...] = ag_part(near_y[0])
        ag_acc[...] += ag_part(near_y[1])
        ag_acc[...] += ag_part(near_y[2])
    g_grad.far(0, 1, 2, 3)
    g_grad.from_core(3)
    with jax.named_scope("attend_grad_last"):
        ag_acc[...] += ag_part(near_y[3])
        for h in range(2):
            ag_st[h] = ag_acc[1 - me.zl, :, h * HEAD : (h + 1) * HEAD].astype(BF16)
            exchange(5 + h, ag_st.at[h], ag_rv.at[h])
    s_out.near((0, 0), (1, 1), (0, 3), (1, 2))
    s_out.to_core(0)
    sends.waits.append(lambda: arrived(s_out.pst, s_out.cs.at[0]))
    s_out.from_core(0)

    for h in range(2):
        own = slice(h * HEAD, (h + 1) * HEAD)
        with jax.named_scope("ag_wait"):
            arrived(ag_rv.at[h], e_rs.at[5 + h])
        with jax.named_scope("backward"):
            a_grad = (tanh_gate * (ag_acc[me.zl, :, own] + ag_rv[h].astype(F32))).astype(BF16)
            attend_grad[h] = a_grad
            prob = probs[h]
            prob_grad = dot(a_grad, value_head, NT)
            delta = jnp.sum(prob * prob_grad, axis=-1, keepdims=True)
            s_grad = (prob * (prob_grad - delta) * scale).astype(BF16)
            score_grad[h] = s_grad
            normed_grad = dot(s_grad, key_head)
            q, q_scale = query[h], query_scale[h]
            mean = jnp.mean(normed_grad * q, axis=-1, keepdims=True)
            q_grad = q_scale * (normed_grad - q * (q_scale * q_scale) * mean)
            dq_g[me.zl, :, own] = q_grad.astype(BF16)
        exchange(7 + h, dq_g.at[me.zl, :, own], dq_g.at[me.zl, :, own])
        if h == 0:
            s_out.near((0, 2), (1, 3))
    with jax.named_scope("kv_part"):
        key_part = dot(score_grad[0], query_low[0], TN) + dot(score_grad[1], query_low[1], TN)
        value_part = dot(probs_low[0], attend_grad[0], TN) + dot(probs_low[1], attend_grad[1], TN)
        kvp[:, :, :HEAD] = key_part.astype(BF16).reshape(4, 64, HEAD)
        kvp[:, :, HEAD:] = value_part.astype(BF16).reshape(4, 64, HEAD)
        for j in range(3):
            p, device = mate(j)
            sends.start(kvp.at[p], kvp_rv.at[piece], n_ss.at[j], n_rs.at[piece], device)

    s_out.start_z(0, 1)

    def text_block(slot, k, cc):
        block = wq_g[slot, pl.ds(pl.multiple_of((k * 2 + cc) * 256, 256), 256), :]
        return dot(dq_g[...].reshape(512, 256), block, NT)

    with jax.named_scope("dq_wait"):
        for h in range(2):
            theirs = dq_g.at[1 - me.zl, :, pl.ds(h * HEAD, HEAD)]
            arrived(theirs, e_rs.at[7 + h])
    s_text = Scatter(me, sends, text_block, acc_t, t_bufs, r_sems[1])
    s_text.to_core(3)
    s_text.to_core(2)
    s_text.from_core(3)
    s_text.send_far(0, 1)

    s_text.to_core(1)
    s_text.from_core(2)
    s_text.near((0, 1))
    s_text.from_core(1)
    s_text.near((1, 0), (0, 0), (1, 1))
    s_text.send_far(2, 3)
    s_text.near((0, 3), (1, 2))
    s_text.to_core(0)
    sends.waits.append(lambda: arrived(s_text.pst, s_text.cs.at[0]))

    with jax.named_scope("kv_grad"):
        kv_grad = kvp[piece].astype(F32)
        for j in range(3):
            p, _ = mate(j)
            arrived(kvp_rv.at[p], n_rs.at[p])
            kv_grad = kv_grad + kvp_rv[p].astype(F32)
        keys = own_kv[:, :HEAD]
        key_scale = lax.rsqrt(jnp.mean(keys * keys, axis=-1, keepdims=True) + EPS)
        k_grad = kv_grad[:, :HEAD]
        mean = jnp.mean(k_grad * keys, axis=-1, keepdims=True)
        k_grad = key_scale * k_grad - keys * (key_scale * key_scale * key_scale) * mean
        jg[:, :HEAD] = k_grad.astype(BF16)
        jg[:, HEAD:] = kv_grad[:, HEAD:].astype(BF16)
        g_kv.direct_z()

    s_out.start_z(2, 3)
    s_text.from_core(0)
    s_text.start_z(0, 1)
    s_text.near((0, 2), (1, 3))
    g_kv.arrive(0, 1, 2, 3, relay=False)
    g_kv.start_y(0, 1, 2, 3)
    g_kv.near(0, 1, 2, 3)
    s_text.start_z(2, 3)
    g_kv.far(0, 1, 2, 3)
    g_kv.from_core(0, 1, 2, 3)

    with jax.named_scope("vision_grad"):
        gv = None
        for i in range(4):
            term = dot(kvg_g[i].reshape(512, 256), wkv_g[i], NT)
            gv = term if gv is None else gv + term
        gv_acc[...] = gv.reshape(4, 2, 64, -1)
        gv_st[...] = gv_acc[:, 1 - me.zl].astype(BF16)
        exchange(9, gv_st, gv_rv)
    with jax.named_scope("update"):
        update[...] = (tanh_gate * s_out.total()).astype(BF16)
    with jax.named_scope("vision_grad_last"):
        arrived(gv_rv, e_rs.at[9])
        total = gv_acc[:, me.zl] + gv_rv[...].astype(F32)
        grad_vision[...] = total.reshape(256, -1).T.astype(BF16)
    with jax.named_scope("text_grad_last"):
        grad_text[...] = s_text.total().astype(BF16)
    with jax.named_scope("sends"):
        sends.finish()


def hand_on(*refs):
    for n in range(3):
        refs[3 + n][...] = refs[n][...]


def body(text, grad_out, vision, gate, w_query, w_key, w_value, w_out):
    features = vision.shape[1]
    dma = lambda n: pltpu.SemaphoreType.DMA((n,))
    vm = pltpu.VMEM

    def scatter_bufs(m):
        return [
            vm((8, 2 * m, 256), BF16), vm((8, 2 * m, 256), BF16),
            vm((4, m, 256), BF16), vm((4, m, 256), BF16),
            vm((8, m, 256), BF16), vm((8, m, 256), BF16),
            vm((4, m, 256), BF16), vm((8 if m == 64 else 5, m, 256), BF16),
        ]

    scratch = [
        vm((4, features, 256), BF16), vm((4, 1024, 256), BF16), vm((4, 256, 1024), BF16),
        vm((4, 2, 2, 2, 256, 256), BF16), vm((4, 2, 2, 2, 256, 256), BF16), vm((4, 2, 2, 2, 64, 256), BF16),
        vm((features, 256), BF16), vm((4, 2, 64, features), BF16),
        vm((2, 256, 256), F32), vm((2, 256, HEAD), BF16), vm((2, 256, HEAD), BF16),
        vm((2, 256, 256), BF16), vm((2, 256, 256), BF16),
        vm((2, 256, 256), F32), vm((2, 256, HEAD), BF16), vm((2, 256, HEAD), BF16),
        vm((4, 2, 64, features), F32), vm((4, 64, features), BF16), vm((4, 64, features), BF16),
        vm((64, 256), BF16), vm((4, 64, 256), BF16), vm((4, 64, 256), BF16), vm((4, 64, 256), BF16),
        vm((2, 256, 256), BF16), vm((2, 256, 256), F32),
        vm((2, 256, HEAD), F32), vm((2, 256, HEAD), BF16), vm((2, 256, HEAD), F32),
        vm((2, 256, HEAD), BF16), vm((2, 256, 256), BF16),
        vm((8, 2, 256, 256), F32), vm((8, 2, 256, 256), F32), vm((8, 2, 64, 256), F32), vm((64, 256), F32),
    ]
    scratch += scatter_bufs(256) + scatter_bufs(256) + scatter_bufs(64)
    scratch += [dma(4), dma(4)] * 3
    scratch += [dma(4), dma(4), dma(4), dma(12), dma(1), dma(4)] * 3
    scratch += [dma(1), dma(4), dma(12), dma(12), dma(8), dma(8)] * 3
    scratch += [dma(10), dma(10), dma(2), dma(2), dma(3), dma(4), dma(2)]
    whole = pl.BlockSpec(memory_space=pltpu.VMEM)
    hbm = pl.BlockSpec(memory_space=pl.ANY)
    update, grad_text, grad_vision = pl.pallas_call(
        kernel,
        out_shape=(
            jax.ShapeDtypeStruct((256, 256), BF16),
            jax.ShapeDtypeStruct((256, 256), BF16),
            jax.ShapeDtypeStruct((features, 256), BF16),
        ),
        in_specs=[hbm, hbm, whole, whole, hbm, whole, whole, hbm],
        out_specs=(whole,) * 3,
        scratch_shapes=scratch,
        name="cross_attention",
        compiler_params=pltpu.CompilerParams(
            collective_id=0, has_side_effects=True, vmem_limit_bytes=60 * 2**20
        ),
    )(
        text, grad_out, vision.T, gate.reshape(1, 1),
        w_query, w_key, w_value, w_out,
    )
    update, grad_text, grad_vision = pl.pallas_call(
        hand_on,
        out_shape=(update, grad_text, grad_vision),
        in_specs=[whole] * 3,
        out_specs=(whole,) * 3,
        name="hand_on",
    )(update, grad_text, grad_vision)
    return update, grad_text, grad_vision.T


def solution(mesh):
    return jax.shard_map(
        body,
        mesh=mesh,
        in_specs=(
            P("dp", "tensor"), P("dp", "tensor"), P("dp", "tensor"), P(),
            P("dp", "tensor"), P("tensor", "dp"), P("tensor", "dp"), P("tensor", "dp"),
        ),
        out_specs=(P("dp", "tensor"), P("dp", "tensor"), P("dp", "tensor")),
        check_vma=False,
    )
```

```python
import jax
import jax.numpy as jnp
from jax import lax
from jax.experimental import pallas as pl
from jax.experimental.pallas import tpu as pltpu
from jax.sharding import PartitionSpec as P

HEAD = 128
EPS = 1e-05
MESH = pl.DeviceIdType.MESH
F32 = jnp.float32
BF16 = jnp.bfloat16
OFFSETS = (0, 3, 1, 2)
NT = (((1,), (1,)), ((), ()))
TN = (((0,), (0,)), ((), ()))


def dot(a, b, dims=(((1,), (0,)), ((), ()))):
    return lax.dot_general(a, b, dims, preferred_element_type=F32)


class Here:
    def __init__(self):
        d, t = lax.axis_index("dp"), lax.axis_index("tensor")
        self.x, self.zl = d // 2, d % 2
        self.y, self.zh, self.c = t // 8, (t // 2) % 4, t % 2
        self.z = 2 * self.zh + self.zl
        self.half = self.zh // 2
        self.kept = self.zl == self.half
        self.place = jnp.where(self.zl == 0, self.z, 7 - self.z) // 2
        self.next_z = (self.z + jnp.where(self.place == 2, 2, -2) * (1 - 2 * self.zl)) % 8
        self.toward = 1 - 2 * self.half

    def order(self, i):
        u = self.place
        table = ((0, 1, 2, 3), (2, 1, 3, 0), (3, 2, 0, 1), (0, 1, 2, 3))
        j = table[3][i]
        for n in (2, 1, 0):
            j = jnp.where(u == n, table[n][i], j)
        return jnp.where(self.zl == 0, j, 3 - j)

    def at(self, dx=0, dy=0, z=None, c=None):
        x = (self.x + dx) % 4 if dx else self.x
        y = (self.y + dy) % 4 if dy else self.y
        z = self.z if z is None else z
        c = self.c if c is None else c
        return (x * 2 + z % 2, y * 8 + (z // 2) * 2 + c)


def rcopy(src, dst, send, recv, device):
    return pltpu.make_async_remote_copy(
        src_ref=src, dst_ref=dst, send_sem=send, recv_sem=recv, device_id=device, device_id_type=MESH
    )


class Sends:
    def __init__(self):
        self.waits = []

    def start(self, *args):
        copy = rcopy(*args)
        copy.start()
        self.waits.append(copy.wait_send)

    def start_if(self, cond, *args):
        @pl.when(cond)
        def _():
            rcopy(*args).start()

        def finish():
            @pl.when(cond)
            def _():
                rcopy(*args).wait_send()

        self.waits.append(finish)

    def finish(self):
        for wait in self.waits:
            wait()


def arrived(dst, sem):
    pltpu.make_async_copy(dst, dst, sem).wait()


class RingGather:
    def __init__(self, me, sends, own, buf, cut, sems):
        self.me, self.sends, self.own, self.buf, self.cut = me, sends, own, buf, cut
        self.ss, self.rs = sems

    def start(self):
        me = self.me
        for way, dx in enumerate((1, -1)):
            self.sends.start(self.own, self.buf.at[me.x], self.ss.at[way], self.rs.at[way], me.at(dx=dx))

    def part(self, slot, way):
        rows = self.buf.shape[1]
        lo, n = ((0, self.cut), (self.cut, rows - self.cut))[way]
        return self.buf.at[slot, pl.ds(lo, n)]

    def relay(self, way):
        me, dx = self.me, (1, -1)[way]
        slot = (me.x - dx) % 4
        arrived(self.buf.at[slot], self.rs.at[way])
        block = self.part(slot, way)
        self.sends.start(block, block, self.ss.at[2 + way], self.rs.at[2 + way], me.at(dx=dx))

    def finish(self):
        for way in range(2):
            arrived(self.part((self.me.x + 2) % 4, way), self.rs.at[2 + way])


class Gather:
    def __init__(self, me, sends, own, buf, sems):
        self.me, self.sends, self.own, self.buf = me, sends, own, buf
        self.zs, self.zr, self.ys, self.yr, self.cs, self.cr = sems

    def start_z(self):
        me = self.me
        dst = self.buf.at[me.y, me.zh % 2, me.c, me.zl]
        recv = self.zr.at[(me.zh % 2) * 2 + me.zl]
        one = me.toward * jnp.where(me.kept, -2, 1)
        args = [
            (self.own, dst, self.zs.at[i], recv, me.at(z=(me.z + sign * one) % 8)) for i, sign in enumerate((1, -1))
        ]
        for arg in args:
            self.sends.start(*arg)

        @pl.when(me.kept)
        def _():
            pltpu.make_async_copy(self.own, dst, recv).start()

    def direct_z(self):
        me = self.me
        dst = self.buf.at[me.y, me.zh % 2, me.c, me.zl]
        recv = self.zr.at[(me.zh % 2) * 2 + me.zl]
        for i in range(4):
            z = me.half + 2 * i
            self.sends.start_if(z != me.z, self.own, dst, self.zs.at[i], recv, me.at(z=z))

        @pl.when(me.kept)
        def _():
            pltpu.make_async_copy(self.own, dst, recv).start()

    def relay_z(self, i):
        if i == 3:
            return
        me = self.me
        cond = (me.place >= 2, me.place != 1, me.place == 1)[i]
        block, sem = self.block(me.y, i), self.zs.at[2 + i % 2]
        args = block, block, sem, self.zr.at[me.order(i)], me.at(z=me.next_z)

        self.sends.start_if(cond, *args)

    def block(self, slot, i):
        j = self.me.order(i)
        return self.buf.at[slot, j // 2, self.me.c, j % 2]

    def to_core(self, slot, r, i):
        block = self.block(slot, i)
        rcopy(block, block, self.cs.at[0], self.cr.at[r], self.me.at(c=1 - self.me.c)).start()

    def arrive(self, *positions, relay=True):
        for i in positions:
            arrived(self.block(self.me.y, i), self.zr.at[self.me.order(i)])
            if relay:
                self.relay_z(i)

    def start_y(self, *positions):
        me = self.me
        for i in positions:
            block = self.block(me.y, i)
            for way, dy in enumerate((1, -1)):
                rcopy(block, block, self.ys.at[way], self.yr.at[way * 4 + i], me.at(dy=dy)).start()
            self.to_core(me.y, 0, i)

    def near(self, *positions):
        me = self.me
        for i in positions:
            for way, dy in enumerate((1, -1)):
                slot = (me.y - dy) % 4
                block = self.block(slot, i)
                arrived(block, self.yr.at[way * 4 + i])
                if way == i % 2:
                    rcopy(block, block, self.ys.at[2 + way], self.yr.at[8 + i], me.at(dy=dy)).start()
                self.to_core(slot, 1 + way, i)

    def far(self, *positions):
        slot = (self.me.y + 2) % 4
        for i in positions:
            arrived(self.block(slot, i), self.yr.at[8 + i])
            self.to_core(slot, 3, i)

    def from_core(self, *rs):
        me = self.me
        for r in rs:
            arrived(self.buf.at[(me.y + OFFSETS[r]) % 4, :, 1 - me.c], self.cr.at[r])
        if 3 in rs:
            self.sends.waits.append(self.sent)

    def sent(self):
        c = self.me.c
        arrived(self.buf.at[:, :, c], self.cs.at[0])
        for way in range(2):
            arrived(self.buf.at[0, :, c], self.ys.at[way])
            arrived(self.buf.at[0, 0, c], self.ys.at[2 + way])


class Scatter:
    def __init__(self, me, sends, compute, acc, bufs, sems):
        self.me, self.sends, self.compute, self.acc = me, sends, compute, acc
        self.pst, self.prv, self.fst, self.frv, self.nst, self.nrv, self.zst, self.zrv = bufs
        self.cs, self.cr, self.ys, self.yr, self.zs, self.zr = sems

    def to_core(self, *rs):
        me = self.me
        for r in rs:

            def step(k, _):
                s = r * 2 + k
                self.pst[s] = self.compute((me.y + OFFSETS[r]) % 4, k, 1 - me.c).astype(BF16)
                rcopy(self.pst.at[s], self.prv.at[s], self.cs.at[0], self.cr.at[r], me.at(c=1 - me.c)).start()
                return 0

            lax.fori_loop(0, 2, step, 0)

    def from_core(self, r):
        me = self.me
        arrived(self.prv.at[pl.ds(r * 2, 2)], self.cr.at[r])

        def step(k, _):
            s = r * 2 + k
            value = self.compute((me.y + OFFSETS[r]) % 4, k, me.c) + self.prv[s].astype(F32)
            self.acc[s] = value.reshape(self.acc.shape[1:])
            return 0

        lax.fori_loop(0, 2, step, 0)

    def mine(self, r, i):
        j = self.me.order(3 - i)
        return self.acc[r * 2 + j // 2, j % 2]

    def send_far(self, *positions):
        for i in positions:
            self.fst[i] = self.mine(3, i).astype(BF16)
            self.sends.start(
                self.fst.at[i], self.frv.at[i], self.ys.at[8 + i], self.yr.at[8 + i], self.me.at(dy=(1, -1)[i % 2])
            )

    def near(self, *items):
        me = self.me
        for way, i in items:
            s = way * 4 + i
            value = self.mine(2 - way, i)
            if i % 2 == way:
                arrived(self.frv.at[i], self.yr.at[8 + i])
                value = value + self.frv[i].astype(F32)
            self.nst[s] = value.astype(BF16)
            self.sends.start(self.nst.at[s], self.nrv.at[s], self.ys.at[s], self.yr.at[s], me.at(dy=(1, -1)[way]))

    def z_args(self, i):
        me = self.me
        slot = jnp.minimum(me.place, 2)
        z = 4 * me.zl + me.order(3 - i)
        if i < 2:
            passes = me.place >= 2
            slot = jnp.where(passes, 1 + (me.place, 5 - me.place)[i], slot)
            z = jnp.where(passes, me.next_z, z)
        return self.zst.at[i], self.zrv.at[slot], self.zs.at[i], self.zr.at[slot], me.at(z=z)

    def start_z(self, *positions):
        me = self.me
        for i in positions:
            total = self.mine(0, i)
            for way in range(2):
                s = way * 4 + i
                arrived(self.nrv.at[s], self.yr.at[s])
                total = total + self.nrv[s].astype(F32)
            self.zst[i] = total.astype(BF16)
            if i >= 2:

                @pl.when(me.place >= 2)
                def _():
                    arrived(self.zrv.at[1 + i], self.zr.at[1 + i])
                    self.zst[i] = (total + self.zrv[1 + i].astype(F32)).astype(BF16)

            args = self.z_args(i)
            if i < 3:
                self.sends.start(*args)
            else:
                self.sends.start_if(jnp.logical_not(me.kept), *args)

                @pl.when(me.kept)
                def _():
                    pltpu.make_async_copy(args[0], args[1], args[3]).start()

    def total(self):
        value = None
        for s in range(3):
            arrived(self.zrv.at[s], self.zr.at[s])
            term = self.zrv[s].astype(F32)
            value = term if value is None else value + term
        return value

    def both_z(self, *positions):
        me = self.me
        for i in positions:
            total = self.mine(0, i)
            for way in range(2):
                s = way * 4 + i
                arrived(self.nrv.at[s], self.yr.at[s])
                total = total + self.nrv[s].astype(F32)
            self.zst[i] = total.astype(BF16)
            j = me.order(3 - i)
            there = (j // 2) * 4 + me.zh
            for k in range(2):
                z = 4 * me.zl + 2 * k + j % 2
                args = self.zst.at[i], self.zrv.at[there], self.zs.at[i * 2 + k], self.zr.at[there], me.at(z=z)
                self.sends.start_if(z != me.z, *args)
                local = pltpu.make_async_copy(*args[:2], args[3])
                pl.when(z == me.z)(local.start)

    def both_total(self, k):
        value = None
        for s in range(4):
            arrived(self.zrv.at[k * 4 + s], self.zr.at[k * 4 + s])
            term = self.zrv[k * 4 + s].astype(F32)
            value = term if value is None else value + term
        return value


def kernel(
    text, grad_out, vision, gate, w_query, w_key, w_value, w_out, update, grad_text, grad_vision,
    wkv_g, wq_g, wo_g, text_g, grad_g, kvg_g, vis_g, vis_r,
    q_acc, q_st, q_rv, att_g, dq_g, ag_acc, ag_st, ag_rv, gv_acc, gv_st, gv_rv, jg, kv_all, kvp, kvp_rv,
    probs_low, probs, query, query_low, query_scale, attend_grad, score_grad, acc_o, acc_t, acc_v, own_kv,
    *rest,
):
    o_bufs, t_bufs, v_bufs = rest[0:8], rest[8:16], rest[16:24]
    rest = rest[24:]
    x_sems = [rest[2 * i : 2 * i + 2] for i in range(3)]
    rest = rest[6:]
    g_sems = [rest[6 * i : 6 * i + 6] for i in range(3)]
    rest = rest[18:]
    r_sems = [rest[6 * i : 6 * i + 6] for i in range(3)]
    rest = rest[18:]
    e_ss, e_rs, m_ss, m_rs, n_ss, n_rs, l_sem = rest

    me = Here()
    sends = Sends()
    zp = me.zl + 2 * me.zh + 1 - 2 * me.zl
    piece = (me.zh % 2) * 2 + me.c
    near_y = [(me.y + off) % 4 for off in OFFSETS]

    def exchange(i, src, dst):
        sends.start(src, dst, e_ss.at[i], e_rs.at[i], me.at(z=zp))

    def mate(j):
        p = (piece + 1 + j) % 4
        return p, me.at(z=me.half * 4 + (p // 2) * 2 + me.zl, c=p % 2)

    gx_kv = RingGather(me, sends, wkv_g.at[me.x], wkv_g, 128, x_sems[0])
    gx_q = RingGather(me, sends, w_query, wq_g, 512, x_sems[1])
    gx_o = RingGather(me, sends, w_out, wo_g, 128, x_sems[2])
    g_text = Gather(me, sends, text, text_g, g_sems[0])
    g_grad = Gather(me, sends, grad_out, grad_g, g_sems[1])
    g_kv = Gather(me, sends, jg, kvg_g, g_sems[2])

    barrier = pltpu.get_barrier_semaphore()
    around = [me.at(dx=1), me.at(dx=-1), me.at(dy=1), me.at(dy=-1), me.at(z=zp)]
    around += [mate(j)[1] for j in range(3)]
    for device in around:
        pl.semaphore_signal(barrier, inc=1, device_id=device, device_id_type=MESH)
    for i in range(4):
        for z in (me.half + 2 * i, 4 * me.zl + i):

            @pl.when(z != me.z)
            def _():
                pl.semaphore_signal(barrier, inc=1, device_id=me.at(z=z), device_id_type=MESH)

    @pl.when(jnp.logical_not(me.kept))
    def _():
        pl.semaphore_signal(barrier, inc=1, device_id=me.at(z=me.next_z), device_id_type=MESH)

    local_q = pltpu.make_async_copy(w_query, wq_g.at[me.x], l_sem.at[0])
    local_o = pltpu.make_async_copy(w_out, wo_g.at[me.x], l_sem.at[1])
    local_q.start()
    local_o.start()
    wkv_g[me.x, :, :HEAD] = w_key[...]
    wkv_g[me.x, :, HEAD:] = w_value[...]
    pl.semaphore_wait(barrier, jnp.where(me.kept, 14, 17))

    g_text.start_z()
    gx_kv.start()
    exchange(0, vision, vis_g)

    def kv_block(slot, k, cc):
        return dot(vis_r[k * 2 + cc].reshape(128, vis_r.shape[3]), wkv_g[slot])

    @pl.when(me.kept)
    def _():
        arrived(g_text.block(me.y, 0), g_text.zr.at[me.order(0)])
        g_text.start_y(0)

    vis_r[:, me.zl] = vision[...].T.reshape(4, 64, -1)
    gx_kv.relay(0)
    gx_kv.relay(1)
    gx_q.start()

    @pl.when(jnp.logical_not(me.kept))
    def _():
        arrived(g_text.block(me.y, 0), g_text.zr.at[me.order(0)])
        g_text.start_y(0)

    g_text.relay_z(0)
    g_text.arrive(1)
    g_text.start_y(1)
    g_text.near(0)
    g_text.arrive(2)
    g_text.start_y(2)
    with jax.named_scope("vis_wait"):
        arrived(vis_g, e_rs.at[0])
    vis_r[:, 1 - me.zl] = vis_g[...].T.reshape(4, 64, -1)
    gx_kv.finish()
    s_kv = Scatter(me, sends, kv_block, acc_v, v_bufs, r_sems[2])
    s_kv.to_core(3, 2, 1, 0)
    sends.waits.append(lambda: arrived(s_kv.pst, s_kv.cs.at[0]))
    g_text.near(1)
    g_text.arrive(3)
    g_text.start_y(3)
    g_grad.start_z()
    s_kv.from_core(3)
    s_kv.send_far(0, 1, 2, 3)
    s_kv.from_core(2)
    s_kv.from_core(1)
    s_kv.near((0, 1), (1, 0), (0, 3), (1, 2))
    s_kv.from_core(0)
    g_text.near(2)
    gx_q.relay(0)
    gx_q.relay(1)
    gx_o.start()
    s_kv.near((0, 0), (1, 1), (0, 2), (1, 3))
    g_text.near(3)
    g_grad.arrive(0)
    g_grad.start_y(0)
    s_kv.both_z(0, 1, 2, 3)
    g_text.far(0, 1, 2, 3)
    g_grad.arrive(1)
    g_grad.start_y(1)
    g_text.from_core(0, 1, 2)
    def q_part(slot):
        total = None
        for j in range(4):
            term = dot(text_g[slot, j // 2, j % 2].reshape(512, 256), wq_g[slot, pl.ds(j * 256, 256), :])
            total = term if total is None else total + term
        return total.reshape(2, 256, 256)

    local_q.wait()
    gx_q.finish()
    with jax.named_scope("query"):
        q_acc[...] = q_part(near_y[0])
        q_acc[...] += q_part(near_y[1])
        q_acc[...] += q_part(near_y[2])
    g_grad.arrive(2)
    g_grad.start_y(2)
    g_text.from_core(3)
    with jax.named_scope("query_last"):
        q_acc[...] += q_part(near_y[3])
        for h in range(2):
            q_st[h] = q_acc[1 - me.zl, :, h * HEAD : (h + 1) * HEAD].astype(BF16)
            exchange(1 + h, q_st.at[h], q_rv.at[h])
    g_grad.arrive(3)
    g_grad.start_y(3)
    g_grad.near(0)
    gx_o.relay(0)
    gx_o.relay(1)
    with jax.named_scope("kv"):
        rows = []
        for k in range(2):
            projected = s_kv.both_total(k)
            rows.append(projected)
            keys = projected[:, :HEAD]
            key_scale = lax.rsqrt(jnp.mean(keys * keys, axis=-1, keepdims=True) + EPS)
            p = k * 2 + me.c
            kv_all[p, :, :HEAD] = (keys * key_scale).astype(BF16)
            kv_all[p, :, HEAD:] = projected[:, HEAD:].astype(BF16)
            sends.start(kv_all.at[p], kv_all.at[p], m_ss.at[k], m_rs.at[k], me.at(c=1 - me.c))
        own_kv[...] = jnp.where(me.zh % 2 == 0, rows[0], rows[1])

    g_grad.near(1)
    with jax.named_scope("kv_wait"):
        for k in range(2):
            arrived(kv_all.at[k * 2 + 1 - me.c], m_rs.at[k])
    kv = kv_all[...].reshape(256, 256)
    key_head, value_head = kv[:, :HEAD], kv[:, HEAD:]
    scale = HEAD ** (-0.5)
    tanh_gate = jnp.tanh(gate[...])

    for h in range(2):
        own = slice(h * HEAD, (h + 1) * HEAD)
        with jax.named_scope("q_wait"):
            arrived(q_rv.at[h], e_rs.at[1 + h])
        with jax.named_scope("attention"):
            q = q_acc[me.zl, :, own] + q_rv[h].astype(F32)
            q_scale = lax.rsqrt(jnp.mean(q * q, axis=-1, keepdims=True) + EPS)
            q_normed = (q * q_scale).astype(BF16)
            query[h] = q
            query_low[h] = q_normed
            query_scale[h] = jnp.broadcast_to(q_scale, q.shape)
            expo = jnp.exp(dot(q_normed, key_head, NT) * scale)
            prob = expo / jnp.sum(expo, axis=-1, keepdims=True)
            probs[h] = prob
            low = prob.astype(BF16)
            probs_low[h] = low
            att_g[me.zl, :, own] = dot(low, value_head).astype(BF16)
            exchange(3 + h, att_g.at[me.zl, :, own], att_g.at[me.zl, :, own])
        g_grad.near(2 + h)

    def ag_part(slot):
        total = None
        for j in range(4):
            term = dot(grad_g[slot, j // 2, j % 2].reshape(512, 256), wo_g[slot, :, pl.ds(j * 256, 256)], NT)
            total = term if total is None else total + term
        return total.reshape(2, 256, 256)

    local_o.wait()
    gx_o.finish()

    def out_block(slot, k, cc):
        block = wo_g[slot, :, pl.ds(pl.multiple_of((k * 2 + cc) * 256, 256), 256)]
        return dot(att_g[...].reshape(512, 256), block)

    with jax.named_scope("att_wait"):
        for h in range(2):
            theirs = att_g.at[1 - me.zl, :, pl.ds(h * HEAD, HEAD)]
            arrived(theirs, e_rs.at[3 + h])
    s_out = Scatter(me, sends, out_block, acc_o, o_bufs, r_sems[0])
    s_out.to_core(3)
    s_out.to_core(2)
    s_out.from_core(3)
    s_out.send_far(0, 1)
    s_out.to_core(1)
    s_out.from_core(2)
    s_out.near((0, 1))
    s_out.from_core(1)
    s_out.near((1, 0))
    s_out.send_far(2, 3)
    g_grad.from_core(0, 1, 2)
    with jax.named_scope("attend_grad"):
        ag_acc[...] = ag_part(near_y[0])
        ag_acc[...] += ag_part(near_y[1])
        ag_acc[...] += ag_part(near_y[2])
    g_grad.far(0, 1, 2, 3)
    g_grad.from_core(3)
    with jax.named_scope("attend_grad_last"):
        ag_acc[...] += ag_part(near_y[3])
        for h in range(2):
            ag_st[h] = ag_acc[1 - me.zl, :, h * HEAD : (h + 1) * HEAD].astype(BF16)
            exchange(5 + h, ag_st.at[h], ag_rv.at[h])
    s_out.near((0, 0), (1, 1), (0, 3), (1, 2))
    s_out.to_core(0)
    sends.waits.append(lambda: arrived(s_out.pst, s_out.cs.at[0]))
    s_out.from_core(0)

    for h in range(2):
        own = slice(h * HEAD, (h + 1) * HEAD)
        with jax.named_scope("ag_wait"):
            arrived(ag_rv.at[h], e_rs.at[5 + h])
        with jax.named_scope("backward"):
            a_grad = (tanh_gate * (ag_acc[me.zl, :, own] + ag_rv[h].astype(F32))).astype(BF16)
            attend_grad[h] = a_grad
            prob = probs[h]
            prob_grad = dot(a_grad, value_head, NT)
            delta = jnp.sum(prob * prob_grad, axis=-1, keepdims=True)
            s_grad = (prob * (prob_grad - delta) * scale).astype(BF16)
            score_grad[h] = s_grad
            normed_grad = dot(s_grad, key_head)
            q, q_scale = query[h], query_scale[h]
            mean = jnp.mean(normed_grad * q, axis=-1, keepdims=True)
            q_grad = q_scale * (normed_grad - q * (q_scale * q_scale) * mean)
            dq_g[me.zl, :, own] = q_grad.astype(BF16)
        exchange(7 + h, dq_g.at[me.zl, :, own], dq_g.at[me.zl, :, own])
        if h == 0:
            s_out.near((0, 2), (1, 3))
    with jax.named_scope("kv_part"):
        key_part = dot(score_grad[0], query_low[0], TN) + dot(score_grad[1], query_low[1], TN)
        value_part = dot(probs_low[0], attend_grad[0], TN) + dot(probs_low[1], attend_grad[1], TN)
        kvp[:, :, :HEAD] = key_part.astype(BF16).reshape(4, 64, HEAD)
        kvp[:, :, HEAD:] = value_part.astype(BF16).reshape(4, 64, HEAD)
        for j in range(3):
            p, device = mate(j)
            sends.start(kvp.at[p], kvp_rv.at[piece], n_ss.at[j], n_rs.at[piece], device)

    s_out.start_z(0, 1)

    def text_block(slot, k, cc):
        block = wq_g[slot, pl.ds(pl.multiple_of((k * 2 + cc) * 256, 256), 256), :]
        return dot(dq_g[...].reshape(512, 256), block, NT)

    with jax.named_scope("dq_wait"):
        for h in range(2):
            theirs = dq_g.at[1 - me.zl, :, pl.ds(h * HEAD, HEAD)]
            arrived(theirs, e_rs.at[7 + h])
    s_text = Scatter(me, sends, text_block, acc_t, t_bufs, r_sems[1])
    s_text.to_core(3)
    s_text.to_core(2)
    s_text.from_core(3)
    s_text.send_far(0, 1)

    s_text.to_core(1)
    s_text.from_core(2)
    s_text.near((0, 1))
    s_text.from_core(1)
    s_text.near((1, 0), (0, 0), (1, 1))
    s_text.send_far(2, 3)
    s_text.near((0, 3), (1, 2))
    s_text.to_core(0)
    sends.waits.append(lambda: arrived(s_text.pst, s_text.cs.at[0]))

    with jax.named_scope("kv_grad"):
        kv_grad = kvp[piece].astype(F32)
        for j in range(3):
            p, _ = mate(j)
            arrived(kvp_rv.at[p], n_rs.at[p])
            kv_grad = kv_grad + kvp_rv[p].astype(F32)
        keys = own_kv[:, :HEAD]
        key_scale = lax.rsqrt(jnp.mean(keys * keys, axis=-1, keepdims=True) + EPS)
        k_grad = kv_grad[:, :HEAD]
        mean = jnp.mean(k_grad * keys, axis=-1, keepdims=True)
        k_grad = key_scale * k_grad - keys * (key_scale * key_scale * key_scale) * mean
        jg[:, :HEAD] = k_grad.astype(BF16)
        jg[:, HEAD:] = kv_grad[:, HEAD:].astype(BF16)
        g_kv.direct_z()

    s_out.start_z(2, 3)
    s_text.from_core(0)
    s_text.start_z(0, 1)
    s_text.near((0, 2), (1, 3))
    g_kv.arrive(0, 1, 2, 3, relay=False)
    g_kv.start_y(0, 1, 2, 3)
    g_kv.near(0, 1, 2, 3)
    s_text.start_z(2, 3)
    g_kv.far(0, 1, 2, 3)
    g_kv.from_core(0, 1, 2, 3)

    with jax.named_scope("vision_grad"):
        gv = None
        for i in range(4):
            term = dot(kvg_g[i].reshape(512, 256), wkv_g[i], NT)
            gv = term if gv is None else gv + term
        gv_acc[...] = gv.reshape(4, 2, 64, -1)
        gv_st[...] = gv_acc[:, 1 - me.zl].astype(BF16)
        exchange(9, gv_st, gv_rv)
    with jax.named_scope("update"):
        update[...] = (tanh_gate * s_out.total()).astype(BF16)
    with jax.named_scope("vision_grad_last"):
        arrived(gv_rv, e_rs.at[9])
        total = gv_acc[:, me.zl] + gv_rv[...].astype(F32)
        grad_vision[...] = total.reshape(256, -1).T.astype(BF16)
    with jax.named_scope("text_grad_last"):
        grad_text[...] = s_text.total().astype(BF16)
    with jax.named_scope("sends"):
        sends.finish()


def hand_on(*refs):
    for n in range(3):
        refs[3 + n][...] = refs[n][...]


def body(text, grad_out, vision, gate, w_query, w_key, w_value, w_out):
    features = vision.shape[1]
    dma = lambda n: pltpu.SemaphoreType.DMA((n,))
    vm = pltpu.VMEM

    def scatter_bufs(m):
        return [
            vm((8, 2 * m, 256), BF16), vm((8, 2 * m, 256), BF16),
            vm((4, m, 256), BF16), vm((4, m, 256), BF16),
            vm((8, m, 256), BF16), vm((8, m, 256), BF16),
            vm((4, m, 256), BF16), vm((8 if m == 64 else 5, m, 256), BF16),
        ]

    scratch = [
        vm((4, features, 256), BF16), vm((4, 1024, 256), BF16), vm((4, 256, 1024), BF16),
        vm((4, 2, 2, 2, 256, 256), BF16), vm((4, 2, 2, 2, 256, 256), BF16), vm((4, 2, 2, 2, 64, 256), BF16),
        vm((features, 256), BF16), vm((4, 2, 64, features), BF16),
        vm((2, 256, 256), F32), vm((2, 256, HEAD), BF16), vm((2, 256, HEAD), BF16),
        vm((2, 256, 256), BF16), vm((2, 256, 256), BF16),
        vm((2, 256, 256), F32), vm((2, 256, HEAD), BF16), vm((2, 256, HEAD), BF16),
        vm((4, 2, 64, features), F32), vm((4, 64, features), BF16), vm((4, 64, features), BF16),
        vm((64, 256), BF16), vm((4, 64, 256), BF16), vm((4, 64, 256), BF16), vm((4, 64, 256), BF16),
        vm((2, 256, 256), BF16), vm((2, 256, 256), F32),
        vm((2, 256, HEAD), F32), vm((2, 256, HEAD), BF16), vm((2, 256, HEAD), F32),
        vm((2, 256, HEAD), BF16), vm((2, 256, 256), BF16),
        vm((8, 2, 256, 256), F32), vm((8, 2, 256, 256), F32), vm((8, 2, 64, 256), F32), vm((64, 256), F32),
    ]
    scratch += scatter_bufs(256) + scatter_bufs(256) + scatter_bufs(64)
    scratch += [dma(4), dma(4)] * 3
    scratch += [dma(4), dma(4), dma(4), dma(12), dma(1), dma(4)] * 3
    scratch += [dma(1), dma(4), dma(12), dma(12), dma(8), dma(8)] * 3
    scratch += [dma(10), dma(10), dma(2), dma(2), dma(3), dma(4), dma(2)]
    whole = pl.BlockSpec(memory_space=pltpu.VMEM)
    hbm = pl.BlockSpec(memory_space=pl.ANY)
    update, grad_text, grad_vision = pl.pallas_call(
        kernel,
        out_shape=(
            jax.ShapeDtypeStruct((256, 256), BF16),
            jax.ShapeDtypeStruct((256, 256), BF16),
            jax.ShapeDtypeStruct((features, 256), BF16),
        ),
        in_specs=[hbm, hbm, whole, whole, hbm, whole, whole, hbm],
        out_specs=(whole,) * 3,
        scratch_shapes=scratch,
        name="cross_attention",
        compiler_params=pltpu.CompilerParams(
            collective_id=0, has_side_effects=True, vmem_limit_bytes=60 * 2**20
        ),
    )(
        text, grad_out, vision.T, gate.reshape(1, 1),
        w_query, w_key, w_value, w_out,
    )
    update, grad_text, grad_vision = pl.pallas_call(
        hand_on,
        out_shape=(update, grad_text, grad_vision),
        in_specs=[whole] * 3,
        out_specs=(whole,) * 3,
        name="hand_on",
    )(update, grad_text, grad_vision)
    return update, grad_text, grad_vision.T


def solution(mesh):
    return jax.shard_map(
        body,
        mesh=mesh,
        in_specs=(
            P("dp", "tensor"), P("dp", "tensor"), P("dp", "tensor"), P(),
            P("dp", "tensor"), P("tensor", "dp"), P("tensor", "dp"), P("tensor", "dp"),
        ),
        out_specs=(P("dp", "tensor"), P("dp", "tensor"), P("dp", "tensor")),
        check_vma=False,
    )
```
